32 devices in a mesh: groups: 2 (over y), inst: 4 (over z), tp: 4 (over x, core).
Axes of the slice: x: 2, y: 2, z: 4, core: 2. Of those that a mesh axis runs over, the one named last changes fastest.
Arguments:
- hidden: bfloat16 [2, 1024, 8192], P(None, ('groups', 'inst'), 'tp'), parts along dimension 1, may hold values from -6 to 6
- key_matrix: bfloat16 [8192, 1024], P('tp'), may hold values from -0.0625 to 0.0625
- adapter_down_weight: bfloat16 [256, 16, 8192], P('inst', None, 'tp'), may hold values from -0.0625 to 0.0625
- adapter_up_weight: bfloat16 [256, 16, 1024], P('inst', None, 'tp'), may hold values from -1.5 to 1.5
- request_adapter_slot: int32 [1024], P(('groups', 'inst')), parts along dimension 0, may hold values from 0 to 31, as said below
- adapter_pool_rows: int32 [64], P('groups'), parts along dimension 0, may hold values from 0 to 255, as said below
- lengths: int32 [1024], P(('groups', 'inst')), parts along dimension 0, may hold values from 1 to 4095
Outputs:
- new_keys: bfloat16 [2, 1024, 1024], P(None, ('groups', 'inst'), 'tp'), parts along dimension 1
The draws below stay inside these ranges and needn't reach their ends.
There are 2 independent parts, one for each index of `groups`. The reference program is written for one: setup_inputs(seed, part) draws one part's arguments, and reference() takes and returns one part's arrays. A program takes and returns all parts, laid end to end along the dimension named above; an argument that names none is the same for every part. Nothing has to cross between parts.
Inputs may be any that keep to these rules, and one draw needn't show every extreme that they name: `adapter_pool_rows`: adapter in use k lies in the pool rows of instance j = k // 8, that is rows j * 64 to j * 64 + 63; the rows of the pool are held in order by the instances, 64 each; the 32 rows are distinct. `request_adapter_slot`: at most 64 of the 128 requests of one instance use adapters held by one instance, and one instance, the same for all, receives exactly 64 from every instance.
All inputs are finite; a program needn't handle non-finite values.
Results may differ from the reference program's by a relative error of at most 0.0055.
Values may be sent and summed in bfloat16 or wider, within the bound.
A program may use at most 64 MiB of HBM per device.

```python
import jax
import jax.numpy as jnp
from jax import lax

MODEL_WIDTH = 8192
HEAD = 128
ADAPTER_RANK = 16
REQUESTS_PER_UNIT = 128
ADP_INST = 64
ACT_INST = 8
KEY_FEATURES = 1024
REQUEST_TOTAL = 512
ADAPTER_TOTAL = 256
CAP = 64
N_INST = 4


def shuffle_row(row_key):
    return jax.random.permutation(row_key, REQUESTS_PER_UNIT)


def pool_pick(row_key):
    return jax.random.permutation(row_key, ADP_INST)[:ACT_INST]


def draw_request_adapter_slot(key, part):
    key = jax.random.fold_in(key, 11)
    key_hot, key_matrix, key_score, key_order, key_pick = jax.random.split(key, 5)
    hot_owner = jax.random.randint(key_hot, (), 0, N_INST)
    item_count = N_INST * CAP
    owner_items = jnp.repeat(jnp.arange(N_INST, dtype=jnp.int32), CAP)
    owner_weights = jax.random.randint(key_matrix, (N_INST, N_INST), 1, 5)
    noise_draw = jax.random.randint(key_score, (N_INST, item_count), 0, 65536)
    scores = noise_draw * jnp.take(owner_weights, owner_items, axis=1)
    scores = scores * 2048 + jnp.arange(item_count, dtype=jnp.int32)[None, :]
    scores = scores + jnp.where(owner_items == hot_owner, 1 << 30, 0).astype(jnp.int32)[None, :]
    top_vals, top_index = lax.top_k(scores, REQUESTS_PER_UNIT)
    owners = jnp.take(owner_items, top_index)
    orders = jax.vmap(shuffle_row)(jax.random.split(key_order, N_INST))
    owners = jnp.take_along_axis(owners, orders, axis=1)
    picks = jax.random.randint(key_pick, (N_INST, REQUESTS_PER_UNIT), 0, ACT_INST)
    return (owners * ACT_INST + picks).reshape(N_INST * REQUESTS_PER_UNIT).astype(jnp.int32)


def draw_adapter_pool_rows(key, part):
    key = jax.random.fold_in(key, 23)
    local_rows = jax.vmap(pool_pick)(jax.random.split(key, N_INST))
    owner_base = jnp.arange(N_INST, dtype=jnp.int32)[:, None] * ADP_INST
    return (owner_base + local_rows).reshape(N_INST * ACT_INST).astype(jnp.int32)


def place_ends(values, rng, smallest, largest):
    longest = values.shape.index(max(values.shape))
    spots = []
    for shift in (0, 1):
        where = [jax.random.randint(jax.random.fold_in(rng, axis), (), 0, length) for axis, length in enumerate(values.shape)]
        where[longest] = (where[longest] + shift) % values.shape[longest]
        spots.append(tuple(where))
    return values.at[spots[0]].set(smallest).at[spots[1]].set(largest)


def steps_of(stream_key, dims, pieces, smallest, largest):
    def one(dim, parts):
        draws = jax.random.uniform(jax.random.fold_in(jax.random.fold_in(stream_key, 6), dim), (parts,), jnp.float32, smallest / len(pieces), largest / len(pieces))
        return jnp.repeat(jnp.exp(draws), dims[dim] // parts).reshape((-1,) + (1,) * (len(dims) - dim - 1))

    loudness = one(*pieces[0])
    for cut in pieces[1:]:
        loudness = loudness * one(*cut)
    return loudness


def normal_values(key, shape, spread, bound, shards=(), kind=jnp.bfloat16):
    gain = steps_of(key, shape, shards, -0.22, 0.18) if shards else 1.0
    values = jax.random.normal(key, shape, jnp.float32) * spread * gain
    return jnp.minimum(jnp.maximum(values, -bound), bound).astype(kind)


def setup_inputs(seed: int = 0, part: int = 0) -> dict:
    arg_keys = jax.random.split(jax.random.key(seed), 8)
    part_splits = jax.random.split(jax.random.fold_in(arg_keys[7], part), 8)
    hidden = normal_values(part_splits[0], (2, REQUEST_TOTAL, MODEL_WIDTH), 1.0, 6.0, ((1, 4), (2, 4)))
    key_matrix = normal_values(arg_keys[1], (MODEL_WIDTH, KEY_FEATURES), MODEL_WIDTH ** -0.5, 0.0625, ((0, 4),))
    adapter_down_weight = normal_values(arg_keys[2], (ADAPTER_TOTAL, ADAPTER_RANK, MODEL_WIDTH), MODEL_WIDTH ** -0.5, 0.0625, ((0, 4), (2, 4)))
    adapter_up_weight = normal_values(arg_keys[3], (ADAPTER_TOTAL, ADAPTER_RANK, KEY_FEATURES), ADAPTER_RANK ** -0.5, 1.5, ((0, 4), (2, 4)))
    request_adapter_slot = draw_request_adapter_slot(jax.random.fold_in(jax.random.fold_in(arg_keys[7], part), 71), part)
    adapter_pool_rows = draw_adapter_pool_rows(jax.random.fold_in(jax.random.fold_in(arg_keys[7], part), 71), part)
    lengths = place_ends(jax.random.randint(part_splits[6], (REQUEST_TOTAL,), 1, 4096), jax.random.fold_in(part_splits[6], 1), 1, 4095).astype(jnp.int32)
    return {"hidden": hidden, "key_matrix": key_matrix, "adapter_down_weight": adapter_down_weight, "adapter_up_weight": adapter_up_weight, "request_adapter_slot": request_adapter_slot, "adapter_pool_rows": adapter_pool_rows, "lengths": lengths}


adapter_scale = 2.0
rope_theta = 500000.0


def rope_freqs(head_size):
    pair_index = jnp.arange(head_size // 2, dtype=jnp.float32)
    base_freq = rope_theta ** (-2.0 * pair_index / head_size)
    wavelen = 2.0 * jnp.pi / base_freq
    smooth = (8192.0 / wavelen - 1.0) / 3.0
    blended = (1.0 - smooth) * base_freq / 8.0 + smooth * base_freq
    scaled = jnp.where(wavelen > 8192.0, base_freq / 8.0, blended)
    return jnp.where(wavelen < 2048.0, base_freq, scaled)


def apply_rope(values, positions, head_size):
    row_count = values.shape[0]
    head_count = values.shape[1] // head_size
    shaped = values.reshape(row_count, head_count, head_size)
    angles = positions.astype(jnp.float32)[:, None] * rope_freqs(head_size)[None, :]
    cosine = jnp.cos(angles)[:, None, :]
    sine_part = jnp.sin(angles)[:, None, :]
    half_head = head_size // 2
    first_half = shaped[:, :, :half_head]
    second = shaped[:, :, half_head:]
    turned = jnp.concatenate([first_half * cosine - second * sine_part, second * cosine + first_half * sine_part], axis=2)
    return turned.reshape(row_count, head_count * head_size)


def block_update(block_operands):
    block_rows, block_pool, down_table, up_table = block_operands
    down_rows = jnp.take(down_table, block_pool, axis=0).astype(jnp.float32)
    shrink = jnp.einsum("rd,rkd->rk", block_rows.astype(jnp.float32), down_rows).astype(jnp.bfloat16)
    up_rows = jnp.take(up_table, block_pool, axis=0).astype(jnp.float32)
    return jnp.einsum("rk,rkc->rc", shrink.astype(jnp.float32), up_rows).astype(jnp.bfloat16)


def reference(hidden, key_matrix, adapter_down_weight, adapter_up_weight, request_adapter_slot, adapter_pool_rows, lengths):
    pool_row = jnp.take(adapter_pool_rows, request_adapter_slot).astype(jnp.int32)
    pool_by_block = pool_row.reshape(N_INST, REQUESTS_PER_UNIT)
    outputs = []
    for step_index in range(2):
        current_rows = hidden[step_index]
        plain_keys = jnp.dot(current_rows, key_matrix, preferred_element_type=jnp.float32)

        def single_block(block_operands):
            return block_update((block_operands[0], block_operands[1], adapter_down_weight, adapter_up_weight))

        adapter_update = lax.map(single_block, (current_rows.reshape(N_INST, REQUESTS_PER_UNIT, MODEL_WIDTH), pool_by_block))
        adapter_update = adapter_update.reshape(REQUEST_TOTAL, KEY_FEATURES)
        combined = plain_keys + adapter_scale * adapter_update.astype(jnp.float32)
        turned = apply_rope(combined, lengths + step_index, HEAD)
        outputs.append(turned.astype(jnp.bfloat16))
    return jnp.stack(outputs, axis=0)
```

```python
import functools

import jax
import jax.numpy as jnp
import numpy as np
from jax import lax
from jax.experimental import pallas as pl
from jax.experimental.pallas import tpu as pltpu
from jax.sharding import PartitionSpec as P

HEAD = 128
ADAPTER_SCALE = 2.0
ROPE_THETA = 500000.0
MESH_ID = pl.DeviceIdType.MESH


def rope_freqs(head_size):
    pair = np.arange(head_size // 2, dtype=np.float64)
    base = ROPE_THETA ** (-2.0 * pair / head_size)
    wavelen = 2.0 * np.pi / base
    smooth = (8192.0 / wavelen - 1.0) / 3.0
    blended = (1.0 - smooth) * base / 8.0 + smooth * base
    scaled = np.where(wavelen > 8192.0, base / 8.0, blended)
    return np.where(wavelen < 2048.0, base, scaled).astype(np.float32)


def kernel(
    n_inst, n_tp, n_act, rank, pool_rows_ref, slot_ref, len_ref, freq_ref,
    hidden_hbm, key_hbm, down_hbm, up_hbm, out_ref,
    hidden, key, down, up, gath, part, keys_in, score, score_in, cos_tab, sin_tab,
    load_sem, out_right_sem, out_left_sem, in_sem, key_out_sem, key_in_sem, sc_out_sem, sc_in_sem,
):
    me = lax.axis_index("inst")
    tp = lax.axis_index("tp")
    steps, requests, width = hidden.shape
    rows = steps * requests
    local = up.shape[2]
    pool_count = down.shape[0]
    block = n_act * rank

    barrier = pltpu.get_barrier_semaphore()
    for shift in (1, n_inst - 1):
        pl.semaphore_signal(
            barrier, inc=1, device_id={"inst": lax.rem(me + shift, n_inst)}, device_id_type=MESH_ID
        )
    for shift in range(1, n_tp):
        pl.semaphore_signal(
            barrier, inc=1, device_id={"tp": lax.rem(tp + shift, n_tp)}, device_id_type=MESH_ID
        )

    load_down = pltpu.make_async_copy(down_hbm, down, load_sem.at[0])
    load_up = pltpu.make_async_copy(up_hbm, up, load_sem.at[1])
    load_hidden = pltpu.make_async_copy(hidden_hbm, hidden, load_sem.at[2])
    load_key = pltpu.make_async_copy(key_hbm, key, load_sem.at[3])
    load_down.start()
    load_up.start()
    load_hidden.start()
    load_key.start()

    load_down.wait()
    load_up.wait()
    for k in range(n_act):
        row = lax.rem(pool_rows_ref[me * n_act + k], pool_count)
        gath[me, k * rank : (k + 1) * rank, :width] = down[row]
        gath[me, k * rank : (k + 1) * rank, width:] = up[row]

    pl.semaphore_wait(barrier, 2 + n_tp - 1)

    def send_right(owner):
        return pltpu.make_async_remote_copy(
            src_ref=gath.at[owner], dst_ref=gath.at[owner],
            send_sem=out_right_sem.at[owner], recv_sem=in_sem.at[owner],
            device_id={"inst": lax.rem(me + 1, n_inst)}, device_id_type=MESH_ID,
        )

    def send_left(owner):
        return pltpu.make_async_remote_copy(
            src_ref=gath.at[owner], dst_ref=gath.at[owner],
            send_sem=out_left_sem.at[owner], recv_sem=in_sem.at[owner],
            device_id={"inst": lax.rem(me + n_inst - 1, n_inst)}, device_id_type=MESH_ID,
        )

    @pl.when(me + 1 < n_inst)
    def _():
        send_right(me).start()

    @pl.when(me > 0)
    def _():
        send_left(me).start()

    load_hidden.wait()
    load_key.wait()

    def send_keys(shift):
        peer = lax.rem(tp + shift, n_tp)
        return pltpu.make_async_remote_copy(
            src_ref=part.at[shift], dst_ref=keys_in.at[shift],
            send_sem=key_out_sem.at[shift], recv_sem=key_in_sem.at[shift],
            device_id={"tp": peer}, device_id_type=MESH_ID,
        )

    def partial_keys(shift):
        peer = lax.rem(tp + shift, n_tp)
        columns = pl.ds(pl.multiple_of(peer * local, local), local)
        part[shift] = jnp.dot(
            hidden[...].reshape(rows, width), key[:, columns], preferred_element_type=jnp.float32
        )

    for shift in range(1, n_tp):
        partial_keys(shift)
        send_keys(shift).start()
    partial_keys(0)

    slots = jnp.concatenate([slot_ref[...]] * steps, axis=1)

    def add_scores(owner):
        piece = lax.dot_general(
            gath[owner, :, :width], hidden[...].reshape(rows, width),
            (((1,), (1,)), ((), ())), preferred_element_type=jnp.float32,
        )
        total = score[0]
        for k in range(n_act):
            total += jnp.where(
                slots == owner * n_act + k, piece[k * rank : (k + 1) * rank, :], 0.0
            )
        score[0] = total

    score[0] = jnp.zeros((rank, rows), jnp.float32)
    add_scores(me)

    lens = jnp.broadcast_to(len_ref[...].astype(jnp.float32), (HEAD, requests)).T
    lane = lax.broadcasted_iota(jnp.int32, (requests, HEAD), 1)
    for s in range(steps):
        angle = (lens + float(s)) * freq_ref[...]
        sine = jnp.sin(angle)
        cos_tab[s * requests : (s + 1) * requests, :] = jnp.cos(angle)
        sin_tab[s * requests : (s + 1) * requests, :] = jnp.where(lane < HEAD // 2, -sine, sine)

    def step(d, carry):
        low = me - d
        high = me + d

        @pl.when(low >= 0)
        def _():
            send_right(low).wait_recv()

            @pl.when(me + 1 < n_inst)
            def _():
                send_right(low).start()

        @pl.when(high < n_inst)
        def _():
            send_left(high).wait_recv()

            @pl.when(me > 0)
            def _():
                send_left(high).start()

        @pl.when(low >= 0)
        def _():
            add_scores(low)

        @pl.when(high < n_inst)
        def _():
            add_scores(high)

        return carry

    lax.fori_loop(1, n_inst, step, 0)

    def send_score(shift):
        return pltpu.make_async_remote_copy(
            src_ref=score.at[0], dst_ref=score_in.at[shift],
            send_sem=sc_out_sem.at[shift], recv_sem=sc_in_sem.at[shift],
            device_id={"tp": lax.rem(tp + shift, n_tp)}, device_id_type=MESH_ID,
        )

    for shift in range(1, n_tp):
        send_score(shift).start()

    plain = part[0]
    for shift in range(1, n_tp):
        send_keys(shift).wait_recv()
        plain += keys_in[shift]

    shrink = score[0]
    for shift in range(1, n_tp):
        send_score(shift).wait_recv()
        shrink += score_in[shift]
    shrink = shrink.astype(jnp.bfloat16).astype(jnp.float32)

    def add_update(owner, total):
        spread = jnp.concatenate(
            [jnp.where(slots == owner * n_act + k, shrink, 0.0) for k in range(n_act)], axis=0
        )
        return total + lax.dot_general(
            spread.astype(jnp.bfloat16), gath[owner, :, width:],
            (((0,), (0,)), ((), ())), preferred_element_type=jnp.float32,
        )

    update = lax.fori_loop(0, n_inst, add_update, jnp.zeros((rows, local), jnp.float32))
    mixed = plain + ADAPTER_SCALE * update.astype(jnp.bfloat16).astype(jnp.float32)
    for h in range(local // HEAD):
        values = mixed[:, h * HEAD : (h + 1) * HEAD]
        turned = values * cos_tab[...] + pltpu.roll(values, HEAD // 2, 1) * sin_tab[...]
        out_ref[:, :, h * HEAD : (h + 1) * HEAD] = turned.astype(jnp.bfloat16).reshape(
            steps, requests, HEAD
        )

    for shift in range(1, n_tp):
        send_keys(shift).wait_send()
        send_score(shift).wait_send()

    def drain(owner, carry):
        @pl.when((owner <= me) & (me + 1 < n_inst))
        def _():
            send_right(owner).wait_send()

        @pl.when((owner >= me) & (me > 0))
        def _():
            send_left(owner).wait_send()

        return carry

    lax.fori_loop(0, n_inst, drain, 0)


def on_device(
    hidden, key_matrix, down_weight, up_weight, request_slot, pool_rows, lengths
):
    n_inst = lax.axis_size("inst")
    n_tp = lax.axis_size("tp")
    steps, requests, width = hidden.shape
    _, rank, local = up_weight.shape
    n_act = pool_rows.shape[0] // n_inst
    rows = steps * requests
    block = n_act * rank
    freqs = rope_freqs(HEAD)
    vmem = pl.BlockSpec(memory_space=pltpu.VMEM)
    hbm = pl.BlockSpec(memory_space=pl.ANY)
    return pl.pallas_call(
        functools.partial(kernel, n_inst, n_tp, n_act, rank),
        out_shape=jax.ShapeDtypeStruct((steps, requests, local), jnp.bfloat16),
        in_specs=[pl.BlockSpec(memory_space=pltpu.SMEM), vmem, vmem, vmem, hbm, hbm, hbm, hbm],
        out_specs=vmem,
        scratch_shapes=[
            pltpu.VMEM(hidden.shape, jnp.bfloat16),
            pltpu.VMEM(key_matrix.shape, jnp.bfloat16),
            pltpu.VMEM(down_weight.shape, jnp.bfloat16),
            pltpu.VMEM(up_weight.shape, jnp.bfloat16),
            pltpu.VMEM((n_inst, block, width + local), jnp.bfloat16),
            pltpu.VMEM((n_tp, rows, local), jnp.float32),
            pltpu.VMEM((n_tp, rows, local), jnp.float32),
            pltpu.VMEM((1, rank, rows), jnp.float32),
            pltpu.VMEM((n_tp, rank, rows), jnp.float32),
            pltpu.VMEM((rows, HEAD), jnp.float32),
            pltpu.VMEM((rows, HEAD), jnp.float32),
            pltpu.SemaphoreType.DMA((4,)),
            pltpu.SemaphoreType.DMA((n_inst,)),
            pltpu.SemaphoreType.DMA((n_inst,)),
            pltpu.SemaphoreType.DMA((n_inst,)),
            pltpu.SemaphoreType.DMA((n_tp,)),
            pltpu.SemaphoreType.DMA((n_tp,)),
            pltpu.SemaphoreType.DMA((n_tp,)),
            pltpu.SemaphoreType.DMA((n_tp,)),
        ],
        compiler_params=pltpu.CompilerParams(
            collective_id=0, has_side_effects=True, vmem_limit_bytes=48 * 1024 * 1024
        ),
        name="lora_keys",
    )(
        pool_rows,
        request_slot.reshape(1, requests),
        lengths.reshape(1, requests),
        jnp.asarray(np.concatenate([freqs, freqs]).reshape(1, HEAD)),
        hidden,
        key_matrix,
        down_weight,
        up_weight,
    )


def solution(mesh):
    placed = (
        P(None, ("groups", "inst"), "tp"),
        P("tp", None),
        P("inst", None, "tp"),
        P("inst", None, "tp"),
        P(("groups", "inst")),
        P("groups"),
        P(("groups", "inst")),
    )
    return jax.shard_map(
        on_device,
        mesh=mesh,
        in_specs=placed,
        out_specs=P(None, ("groups", "inst"), "tp"),
        check_vma=False,
    )
```

```python
import functools

import jax
import jax.numpy as jnp
import numpy as np
from jax import lax
from jax.experimental import pallas as pl
from jax.experimental.pallas import tpu as pltpu
from jax.sharding import PartitionSpec as P

HEAD = 128
ADAPTER_SCALE = 2.0
ROPE_THETA = 500000.0
MESH_ID = pl.DeviceIdType.MESH


def rope_freqs(head_size):
    pair = np.arange(head_size // 2, dtype=np.float64)
    base = ROPE_THETA ** (-2.0 * pair / head_size)
    wavelen = 2.0 * np.pi / base
    smooth = (8192.0 / wavelen - 1.0) / 3.0
    blended = (1.0 - smooth) * base / 8.0 + smooth * base
    scaled = np.where(wavelen > 8192.0, base / 8.0, blended)
    return np.where(wavelen < 2048.0, base, scaled).astype(np.float32)


def kernel(
    n_inst, n_tp, n_act, rank, pool_rows_hbm, slot_hbm, len_hbm, freq_hbm,
    hidden_hbm, key_hbm, down_hbm, up_hbm, out_ref,
    pool_rows, slot, length, freq, hidden, key, down, up, low_half, high_half, guest, guest_slot,
    part, keys_in, score, help_out, help_in, score_in, cos_tab, sin_tab,
    small_sem, load_sem, out_right_sem, out_left_sem, in_sem, guest_out_sem, guest_in_sem,
    help_out_sem, help_in_sem, key_out_sem, key_in_sem, sc_out_sem, sc_in_sem,
):
    me = lax.axis_index("inst")
    tp = lax.axis_index("tp")
    _, steps, requests, half = hidden.shape
    rows = steps * requests
    local = up.shape[2]
    pool_count = down.shape[0]
    last = n_inst - 1
    is_end = (me == 0) | (me == last)

    load_down = pltpu.make_async_copy(down_hbm, down, load_sem.at[0])
    load_up = pltpu.make_async_copy(up_hbm, up, load_sem.at[1])
    load_hidden = [
        pltpu.make_async_copy(
            hidden_hbm.at[:, :, pl.ds(h * half, half)], hidden.at[h], load_sem.at[2 + h]
        )
        for h in range(2)
    ]
    load_key = pltpu.make_async_copy(key_hbm, key, load_sem.at[4])
    load_small = [
        pltpu.make_async_copy(src, dst, small_sem.at[i])
        for i, (src, dst) in enumerate(
            ((pool_rows_hbm, pool_rows), (slot_hbm, slot), (len_hbm, length), (freq_hbm, freq))
        )
    ]
    for copy in load_small:
        copy.start()
    load_down.start()
    load_up.start()
    for copy in load_hidden:
        copy.start()
    load_key.start()

    barrier = pltpu.get_barrier_semaphore()
    for shift in (1, n_inst - 1):
        pl.semaphore_signal(
            barrier, inc=1, device_id={"inst": lax.rem(me + shift, n_inst)}, device_id_type=MESH_ID
        )
    for shift in range(1, n_tp):
        pl.semaphore_signal(
            barrier, inc=1, device_id={"tp": lax.rem(tp + shift, n_tp)}, device_id_type=MESH_ID
        )

    for copy in load_small:
        copy.wait()
    load_down.wait()
    load_up.wait()
    for k in range(n_act):
        row = lax.rem(pool_rows[me * n_act + k], pool_count)
        ranks = slice(k * rank, (k + 1) * rank)
        low_half[me, ranks, :half] = down[row, :, :half]
        low_half[me, ranks, half:] = up[row]
        high_half[me, ranks, :] = down[row, :, half:]

    pl.semaphore_wait(barrier, 2 + n_tp - 1)

    right = {"inst": lax.rem(me + 1, n_inst)}
    left = {"inst": lax.rem(me + n_inst - 1, n_inst)}

    def remote(src, dst, send_sem, recv_sem, device):
        return pltpu.make_async_remote_copy(
            src_ref=src, dst_ref=dst, send_sem=send_sem, recv_sem=recv_sem,
            device_id=device, device_id_type=MESH_ID,
        )

    def hop(h, owner, sems, device):
        buffer = high_half if h else low_half
        return remote(
            buffer.at[owner], buffer.at[owner], sems.at[h, owner], in_sem.at[h, owner], device
        )

    def go_right(h, owner):
        @pl.when(me + 1 < (last if h else n_inst))
        def _():
            hop(h, owner, out_right_sem, right).start()

    def go_left(h, owner):
        @pl.when(me > (1 if h else 0))
        def _():
            hop(h, owner, out_left_sem, left).start()

    def arrive(h, owner):
        hop(h, owner, out_right_sem, right).wait_recv()

    for h in range(2):
        go_right(h, me)
        go_left(h, me)

    for copy in load_hidden:
        copy.wait()
    load_key.wait()

    def send_keys(shift):
        return remote(
            part.at[shift], keys_in.at[shift], key_out_sem.at[shift], key_in_sem.at[shift],
            {"tp": lax.rem(tp + shift, n_tp)},
        )

    def partial_keys(shift):
        peer = lax.rem(tp + shift, n_tp)
        columns = pl.ds(pl.multiple_of(peer * local, local), local)
        part[shift] = jnp.dot(
            hidden[0].reshape(rows, half), key[:half, columns], preferred_element_type=jnp.float32
        ) + jnp.dot(
            hidden[1].reshape(rows, half), key[half:, columns], preferred_element_type=jnp.float32
        )

    for shift in range(1, n_tp):
        partial_keys(shift)
        send_keys(shift).start()
    partial_keys(0)

    slots = jnp.concatenate([slot[...]] * steps, axis=1)

    def pick(total, weights, values, wanted, owner):
        piece = lax.dot_general(
            weights, values, (((1,), (1,)), ((), ())), preferred_element_type=jnp.float32
        )
        for k in range(n_act):
            total += jnp.where(
                wanted == owner * n_act + k, piece[k * rank : (k + 1) * rank, :], 0.0
            )
        return total

    def add_low(owner):
        score[...] = pick(
            score[...], low_half[owner, :, :half], hidden[0].reshape(rows, half), slots, owner
        )

    def add_high(owner):
        score[...] = pick(
            score[...], high_half[owner], hidden[1].reshape(rows, half), slots, owner
        )

    score[...] = jnp.zeros((rank, rows), jnp.float32)
    add_low(me)
    add_high(me)

    lens = jnp.broadcast_to(length[...].astype(jnp.float32), (HEAD, requests)).T
    lane = lax.broadcasted_iota(jnp.int32, (requests, HEAD), 1)
    for s in range(steps):
        angle = (lens + float(s)) * freq[...]
        sine = jnp.sin(angle)
        cos_tab[s * requests : (s + 1) * requests, :] = jnp.cos(angle)
        sin_tab[s * requests : (s + 1) * requests, :] = jnp.where(lane < HEAD // 2, -sine, sine)

    ends = ((0, 0, 1, right), (1, last, last - 1, left))

    def send_guest(e, device):
        return (
            remote(hidden.at[1], guest.at[e], guest_out_sem.at[e, 0], guest_in_sem.at[e, 0], device),
            remote(slot, guest_slot.at[e], guest_out_sem.at[e, 1], guest_in_sem.at[e, 1], device),
        )

    for e, end, _, device in ends:
        sems = out_left_sem if e else out_right_sem

        @pl.when(me == end)
        def _():
            hop(0, me, sems, device).wait_send()
            if n_inst > 2:
                hop(1, me, sems, device).wait_send()
            for copy in send_guest(e, device):
                copy.start()

    def step(d, carry):
        lower = me - d
        upper = me + d
        sides = ((lower, lower >= 0, go_right), (upper, upper < n_inst, go_left))
        for owner, there, go_on in sides:

            @pl.when(there)
            def _():
                arrive(0, owner)
                go_on(0, owner)

        for owner, there, go_on in sides:

            @pl.when(there & jnp.logical_not(is_end))
            def _():
                arrive(1, owner)
                go_on(1, owner)
                add_high(owner)

        for owner, there, go_on in sides:

            @pl.when(there)
            def _():
                add_low(owner)

        return carry

    lax.fori_loop(1, n_inst, step, 0)

    def send_help(e, device):
        return remote(help_out.at[e], help_in, help_out_sem.at[e], help_in_sem.at[e], device)

    for e, end, helper, device in ends:
        back = left if e == 0 else right

        @pl.when(me == helper)
        def _():
            for copy in send_guest(e, device):
                copy.wait_recv()
            wanted = jnp.concatenate([guest_slot[e]] * steps, axis=1)

            def add_guest(i, total):
                owner = i + 1 - e
                return pick(
                    total, high_half[owner], guest[e].reshape(rows, half), wanted, owner
                )

            help_out[e] = lax.fori_loop(
                0, n_inst - 1, add_guest, jnp.zeros((rank, rows), jnp.float32)
            )
            send_help(e, back).start()

    for e, end, helper, device in ends:

        @pl.when(me == end)
        def _():
            send_help(e, device).wait_recv()
            score[...] += help_in[...]

    def send_score(shift):
        return remote(
            score, score_in.at[shift], sc_out_sem.at[shift], sc_in_sem.at[shift],
            {"tp": lax.rem(tp + shift, n_tp)},
        )

    for shift in range(1, n_tp):
        send_score(shift).start()

    for shift in range(1, n_tp):
        send_keys(shift).wait_recv()
        part[0] += keys_in[shift]

    shrink = score[...]
    for shift in range(1, n_tp):
        send_score(shift).wait_recv()
        shrink += score_in[shift]
    shrink = shrink.astype(jnp.bfloat16).astype(jnp.float32)

    def add_update(owner, total):
        spread = jnp.concatenate(
            [jnp.where(slots == owner * n_act + k, shrink, 0.0) for k in range(n_act)], axis=0
        )
        return total + lax.dot_general(
            spread.astype(jnp.bfloat16), low_half[owner, :, half:],
            (((0,), (0,)), ((), ())), preferred_element_type=jnp.float32,
        )

    update = lax.fori_loop(0, n_inst, add_update, jnp.zeros((rows, local), jnp.float32))
    mixed = part[0] + ADAPTER_SCALE * update.astype(jnp.bfloat16).astype(jnp.float32)
    for h in range(local // HEAD):
        values = mixed[:, h * HEAD : (h + 1) * HEAD]
        turned = values * cos_tab[...] + pltpu.roll(values, HEAD // 2, 1) * sin_tab[...]
        out_ref[:, :, h * HEAD : (h + 1) * HEAD] = turned.astype(jnp.bfloat16).reshape(
            steps, requests, HEAD
        )

    for shift in range(1, n_tp):
        send_keys(shift).wait_send()
        send_score(shift).wait_send()
    for e, end, helper, device in ends:

        @pl.when(me == end)
        def _():
            for copy in send_guest(e, device):
                copy.wait_send()

        @pl.when(me == helper)
        def _():
            send_help(e, device).wait_send()

    def drain(owner, carry):
        for h in range(2):
            @pl.when((owner <= me) & (me + 1 < (last if h else n_inst)) & (me > 0))
            def _():
                hop(h, owner, out_right_sem, right).wait_send()

            @pl.when((owner >= me) & (me > (1 if h else 0)) & (me < last))
            def _():
                hop(h, owner, out_left_sem, left).wait_send()

        return carry

    lax.fori_loop(0, n_inst, drain, 0)


def on_device(
    hidden, key_matrix, down_weight, up_weight, request_slot, pool_rows, lengths
):
    n_inst = lax.axis_size("inst")
    n_tp = lax.axis_size("tp")
    steps, requests, width = hidden.shape
    _, rank, local = up_weight.shape
    n_act = pool_rows.shape[0] // n_inst
    rows = steps * requests
    block = n_act * rank
    freqs = rope_freqs(HEAD)
    half = width // 2
    vmem = pl.BlockSpec(memory_space=pltpu.VMEM)
    hbm = pl.BlockSpec(memory_space=pltpu.HBM)
    return pl.pallas_call(
        functools.partial(kernel, n_inst, n_tp, n_act, rank),
        out_shape=jax.ShapeDtypeStruct((steps, requests, local), jnp.bfloat16),
        in_specs=[hbm] * 8,
        out_specs=vmem,
        scratch_shapes=[
            pltpu.SMEM(pool_rows.shape, jnp.int32),
            pltpu.VMEM((1, requests), jnp.int32),
            pltpu.VMEM((1, requests), jnp.int32),
            pltpu.VMEM((1, HEAD), jnp.float32),
            pltpu.VMEM((2, steps, requests, half), jnp.bfloat16),
            pltpu.VMEM(key_matrix.shape, jnp.bfloat16),
            pltpu.VMEM(down_weight.shape, jnp.bfloat16),
            pltpu.VMEM(up_weight.shape, jnp.bfloat16),
            pltpu.VMEM((n_inst, block, half + local), jnp.bfloat16),
            pltpu.VMEM((n_inst, block, half), jnp.bfloat16),
            pltpu.VMEM((2, steps, requests, half), jnp.bfloat16),
            pltpu.VMEM((2, 1, requests), jnp.int32),
            pltpu.VMEM((n_tp, rows, local), jnp.float32),
            pltpu.VMEM((n_tp, rows, local), jnp.float32),
            pltpu.VMEM((rank, rows), jnp.float32),
            pltpu.VMEM((2, rank, rows), jnp.float32),
            pltpu.VMEM((rank, rows), jnp.float32),
            pltpu.VMEM((n_tp, rank, rows), jnp.float32),
            pltpu.VMEM((rows, HEAD), jnp.float32),
            pltpu.VMEM((rows, HEAD), jnp.float32),
            pltpu.SemaphoreType.DMA((4,)),
            pltpu.SemaphoreType.DMA((5,)),
            pltpu.SemaphoreType.DMA((2, n_inst)),
            pltpu.SemaphoreType.DMA((2, n_inst)),
            pltpu.SemaphoreType.DMA((2, n_inst)),
            pltpu.SemaphoreType.DMA((2, 2)),
            pltpu.SemaphoreType.DMA((2, 2)),
            pltpu.SemaphoreType.DMA((2,)),
            pltpu.SemaphoreType.DMA((2,)),
            pltpu.SemaphoreType.DMA((n_tp,)),
            pltpu.SemaphoreType.DMA((n_tp,)),
            pltpu.SemaphoreType.DMA((n_tp,)),
            pltpu.SemaphoreType.DMA((n_tp,)),
        ],
        compiler_params=pltpu.CompilerParams(
            collective_id=0, has_side_effects=True, vmem_limit_bytes=48 * 1024 * 1024
        ),
        name="lora_keys",
    )(
        pool_rows,
        request_slot.reshape(1, requests),
        lengths.reshape(1, requests),
        jnp.asarray(np.concatenate([freqs, freqs]).reshape(1, HEAD)),
        hidden,
        key_matrix,
        down_weight,
        up_weight,
    )


def solution(mesh):
    placed = (
        P(None, ("groups", "inst"), "tp"),
        P("tp", None),
        P("inst", None, "tp"),
        P("inst", None, "tp"),
        P(("groups", "inst")),
        P("groups"),
        P(("groups", "inst")),
    )
    return jax.shard_map(
        on_device,
        mesh=mesh,
        in_specs=placed,
        out_specs=P(None, ("groups", "inst"), "tp"),
        check_vma=False,
    )
```

```python
import functools

import jax
import jax.numpy as jnp
import numpy as np
from jax import lax
from jax.experimental import pallas as pl
from jax.experimental.pallas import tpu as pltpu
from jax.sharding import PartitionSpec as P

HEAD = 128
ADAPTER_SCALE = 2.0
ROPE_THETA = 500000.0
MESH_ID = pl.DeviceIdType.MESH


def rope_freqs(head_size):
    pair = np.arange(head_size // 2, dtype=np.float64)
    base = ROPE_THETA ** (-2.0 * pair / head_size)
    wavelen = 2.0 * np.pi / base
    smooth = (8192.0 / wavelen - 1.0) / 3.0
    blended = (1.0 - smooth) * base / 8.0 + smooth * base
    scaled = np.where(wavelen > 8192.0, base / 8.0, blended)
    return np.where(wavelen < 2048.0, base, scaled).astype(np.float32)


def kernel(
    n_inst, n_tp, n_act, rank, pool_rows_hbm, slot_hbm, len_hbm, freq_hbm,
    hidden_hbm, key_hbm, down_hbm, up_hbm, out_ref,
    pool_rows, slot, length, freq, hidden, key, down, up, low_half, high_half, guest, guest_slot,
    part, keys_in, score, total_score, help_out, help_in, score_in, cos_tab, sin_tab,
    small_sem, load_sem, out_right_sem, out_left_sem, in_sem, guest_out_sem, guest_in_sem,
    help_out_sem, help_in_sem, key_out_sem, key_in_sem, sc_out_sem, sc_in_sem,
):
    me = lax.axis_index("inst")
    tp = lax.axis_index("tp")
    _, steps, requests, half = hidden.shape
    rows = steps * requests
    local = up.shape[2]
    pool_count = down.shape[0]
    last = n_inst - 1
    is_end = (me == 0) | (me == last)

    load_down = pltpu.make_async_copy(down_hbm, down, load_sem.at[0])
    load_up = pltpu.make_async_copy(up_hbm, up, load_sem.at[1])
    load_hidden = [
        pltpu.make_async_copy(
            hidden_hbm.at[:, :, pl.ds(h * half, half)], hidden.at[h], load_sem.at[2 + h]
        )
        for h in range(2)
    ]
    load_key = pltpu.make_async_copy(key_hbm, key, load_sem.at[4])
    load_small = [
        pltpu.make_async_copy(src, dst, small_sem.at[i])
        for i, (src, dst) in enumerate(
            ((pool_rows_hbm, pool_rows), (slot_hbm, slot), (len_hbm, length), (freq_hbm, freq))
        )
    ]
    for copy in load_small:
        copy.start()
    load_down.start()
    load_up.start()

    barrier = pltpu.get_barrier_semaphore()
    for shift in (1, n_inst - 1):
        pl.semaphore_signal(
            barrier, inc=1, device_id={"inst": lax.rem(me + shift, n_inst)}, device_id_type=MESH_ID
        )
    for shift in range(1, n_tp):
        pl.semaphore_signal(
            barrier, inc=1, device_id={"tp": lax.rem(tp + shift, n_tp)}, device_id_type=MESH_ID
        )

    ends = (
        (0, 0, 1, {"inst": lax.rem(me + 1, n_inst)}),
        (1, last, last - 1, {"inst": lax.rem(me + n_inst - 1, n_inst)}),
    )
    for e, end, helper, _ in ends:
        for here, there in ((end, helper), (helper, end)):

            @pl.when(me == here)
            def _():
                for shift in range(1, n_tp):
                    pl.semaphore_signal(
                        barrier, inc=1, device_id={"inst": there, "tp": lax.rem(tp + shift, n_tp)},
                        device_id_type=MESH_ID,
                    )

    for copy in load_small:
        copy.wait()
    load_down.wait()
    load_up.wait()
    for copy in load_hidden:
        copy.start()
    load_key.start()
    for k in range(n_act):
        row = lax.rem(pool_rows[me * n_act + k], pool_count)
        ranks = slice(k * rank, (k + 1) * rank)
        low_half[me, ranks, :half] = down[row, :, :half]
        low_half[me, ranks, half:] = up[row]
        high_half[me, ranks, :] = down[row, :, half:]

    pairs = 0
    for _, end, helper, _ in ends:
        for here in (end, helper):
            pairs += jnp.where(me == here, 1, 0)
    pl.semaphore_wait(barrier, 2 + (n_tp - 1) * (1 + pairs))

    right = {"inst": lax.rem(me + 1, n_inst)}
    left = {"inst": lax.rem(me + n_inst - 1, n_inst)}

    def remote(src, dst, send_sem, recv_sem, device):
        return pltpu.make_async_remote_copy(
            src_ref=src, dst_ref=dst, send_sem=send_sem, recv_sem=recv_sem,
            device_id=device, device_id_type=MESH_ID,
        )

    def hop(h, owner, sems, device):
        buffer = high_half if h else low_half
        return remote(
            buffer.at[owner], buffer.at[owner], sems.at[h, owner], in_sem.at[h, owner], device
        )

    def go_right(h, owner):
        @pl.when(me + 1 < (last if h else n_inst))
        def _():
            hop(h, owner, out_right_sem, right).start()

    def go_left(h, owner):
        @pl.when(me > (1 if h else 0))
        def _():
            hop(h, owner, out_left_sem, left).start()

    def arrive(h, owner):
        hop(h, owner, out_right_sem, right).wait_recv()

    go_right(0, me)
    go_left(0, me)

    for copy in load_hidden:
        copy.wait()
    load_key.wait()

    def send_keys(shift):
        return remote(
            part.at[shift], keys_in.at[shift], key_out_sem.at[shift], key_in_sem.at[shift],
            {"tp": lax.rem(tp + shift, n_tp)},
        )

    def partial_keys(shift):
        peer = lax.rem(tp + shift, n_tp)
        columns = pl.ds(pl.multiple_of(peer * local, local), local)
        part[shift] = jnp.dot(
            hidden[0].reshape(rows, half), key[:half, columns], preferred_element_type=jnp.float32
        ) + jnp.dot(
            hidden[1].reshape(rows, half), key[half:, columns], preferred_element_type=jnp.float32
        )

    for shift in range(1, n_tp):
        partial_keys(shift)
        send_keys(shift).start()
    partial_keys(0)

    slots = jnp.concatenate([slot[...]] * steps, axis=1)

    def pick(total, weights, values, wanted, owner):
        piece = lax.dot_general(
            weights, values, (((1,), (1,)), ((), ())), preferred_element_type=jnp.float32
        )
        for k in range(n_act):
            total += jnp.where(
                wanted == owner * n_act + k, piece[k * rank : (k + 1) * rank, :], 0.0
            )
        return total

    def add_low(owner):
        score[...] = pick(
            score[...], low_half[owner, :, :half], hidden[0].reshape(rows, half), slots, owner
        )

    def add_high(owner):
        score[...] = pick(
            score[...], high_half[owner], hidden[1].reshape(rows, half), slots, owner
        )

    score[...] = jnp.zeros((rank, rows), jnp.float32)
    add_low(me)
    add_high(me)

    lens = jnp.broadcast_to(length[...].astype(jnp.float32), (HEAD, requests)).T
    lane = lax.broadcasted_iota(jnp.int32, (requests, HEAD), 1)
    for s in range(steps):
        angle = (lens + float(s)) * freq[...]
        sine = jnp.sin(angle)
        cos_tab[s * requests : (s + 1) * requests, :] = jnp.cos(angle)
        sin_tab[s * requests : (s + 1) * requests, :] = jnp.where(lane < HEAD // 2, -sine, sine)

    @pl.when(me < last)
    def _():
        hop(0, me, out_right_sem, right).wait_send()

    go_right(1, me)

    @pl.when(me > 0)
    def _():
        hop(0, me, out_left_sem, left).wait_send()

    go_left(1, me)

    def send_guest(e, device):
        return (
            remote(hidden.at[1], guest.at[e], guest_out_sem.at[e, 0], guest_in_sem.at[e, 0], device),
            remote(slot, guest_slot.at[e], guest_out_sem.at[e, 1], guest_in_sem.at[e, 1], device),
        )

    for e, end, _, device in ends:
        sems = out_left_sem if e else out_right_sem

        @pl.when(me == end)
        def _():
            if n_inst > 2:
                hop(1, me, sems, device).wait_send()
            for copy in send_guest(e, device):
                copy.start()

    def step(d, carry):
        lower = me - d
        upper = me + d
        sides = ((lower, lower >= 0, go_right), (upper, upper < n_inst, go_left))
        for owner, there, go_on in sides:

            @pl.when(there)
            def _():
                arrive(0, owner)
                go_on(0, owner)

        for owner, there, go_on in sides:

            @pl.when(there & jnp.logical_not(is_end))
            def _():
                arrive(1, owner)
                go_on(1, owner)
                add_high(owner)

        for owner, there, go_on in sides:

            @pl.when(there)
            def _():
                add_low(owner)

        return carry

    lax.fori_loop(1, n_inst, step, 0)

    def send_help(e, shift):
        return remote(
            help_out.at[e], help_in.at[shift], help_out_sem.at[e, shift], help_in_sem.at[shift],
            {"inst": ends[e][1], "tp": lax.rem(tp + shift, n_tp)},
        )

    for e, end, helper, device in ends:

        @pl.when(me == helper)
        def _():
            for copy in send_guest(e, device):
                copy.wait_recv()
            wanted = jnp.concatenate([guest_slot[e]] * steps, axis=1)

            def add_guest(i, total):
                owner = i + 1 - e
                return pick(
                    total, high_half[owner], guest[e].reshape(rows, half), wanted, owner
                )

            help_out[e] = lax.fori_loop(
                0, n_inst - 1, add_guest, jnp.zeros((rank, rows), jnp.float32)
            )
            for shift in range(n_tp):
                send_help(e, shift).start()

    def send_score(shift):
        return remote(
            score, score_in.at[shift], sc_out_sem.at[shift], sc_in_sem.at[shift],
            {"tp": lax.rem(tp + shift, n_tp)},
        )

    for shift in range(1, n_tp):
        send_score(shift).start()

    for shift in range(1, n_tp):
        send_keys(shift).wait_recv()
        part[0] += keys_in[shift]

    for shift in range(1, n_tp):
        send_score(shift).wait_recv()
    shrink = score[...]
    for shift in range(1, n_tp):
        shrink += score_in[shift]
    total_score[...] = shrink

    @pl.when(is_end)
    def _():
        for shift in range(n_tp):
            send_help(0, shift).wait_recv()
            total_score[...] += help_in[shift]

    shrink = total_score[...].astype(jnp.bfloat16).astype(jnp.float32)

    def add_update(owner, total):
        spread = jnp.concatenate(
            [jnp.where(slots == owner * n_act + k, shrink, 0.0) for k in range(n_act)], axis=0
        )
        return total + lax.dot_general(
            spread.astype(jnp.bfloat16), low_half[owner, :, half:],
            (((0,), (0,)), ((), ())), preferred_element_type=jnp.float32,
        )

    update = lax.fori_loop(0, n_inst, add_update, jnp.zeros((rows, local), jnp.float32))
    mixed = part[0] + ADAPTER_SCALE * update.astype(jnp.bfloat16).astype(jnp.float32)
    for h in range(local // HEAD):
        values = mixed[:, h * HEAD : (h + 1) * HEAD]
        turned = values * cos_tab[...] + pltpu.roll(values, HEAD // 2, 1) * sin_tab[...]
        out_ref[:, :, h * HEAD : (h + 1) * HEAD] = turned.astype(jnp.bfloat16).reshape(
            steps, requests, HEAD
        )

    for shift in range(1, n_tp):
        send_keys(shift).wait_send()
        send_score(shift).wait_send()
    for e, end, helper, device in ends:

        @pl.when(me == end)
        def _():
            for copy in send_guest(e, device):
                copy.wait_send()

        @pl.when(me == helper)
        def _():
            for shift in range(n_tp):
                send_help(e, shift).wait_send()

    def drain(owner, carry):
        @pl.when((owner < me) & (me < last))
        def _():
            hop(0, owner, out_right_sem, right).wait_send()

        @pl.when((owner > me) & (me > 0))
        def _():
            hop(0, owner, out_left_sem, left).wait_send()

        @pl.when((owner <= me) & (me + 1 < last) & (me > 0))
        def _():
            hop(1, owner, out_right_sem, right).wait_send()

        @pl.when((owner >= me) & (me > 1) & (me < last))
        def _():
            hop(1, owner, out_left_sem, left).wait_send()

        return carry

    lax.fori_loop(0, n_inst, drain, 0)


def on_device(
    hidden, key_matrix, down_weight, up_weight, request_slot, pool_rows, lengths
):
    n_inst = lax.axis_size("inst")
    n_tp = lax.axis_size("tp")
    steps, requests, width = hidden.shape
    _, rank, local = up_weight.shape
    n_act = pool_rows.shape[0] // n_inst
    rows = steps * requests
    block = n_act * rank
    freqs = rope_freqs(HEAD)
    half = width // 2
    vmem = pl.BlockSpec(memory_space=pltpu.VMEM)
    hbm = pl.BlockSpec(memory_space=pltpu.HBM)
    return pl.pallas_call(
        functools.partial(kernel, n_inst, n_tp, n_act, rank),
        out_shape=jax.ShapeDtypeStruct((steps, requests, local), jnp.bfloat16),
        in_specs=[hbm] * 8,
        out_specs=vmem,
        scratch_shapes=[
            pltpu.SMEM(pool_rows.shape, jnp.int32),
            pltpu.VMEM((1, requests), jnp.int32),
            pltpu.VMEM((1, requests), jnp.int32),
            pltpu.VMEM((1, HEAD), jnp.float32),
            pltpu.VMEM((2, steps, requests, half), jnp.bfloat16),
            pltpu.VMEM(key_matrix.shape, jnp.bfloat16),
            pltpu.VMEM(down_weight.shape, jnp.bfloat16),
            pltpu.VMEM(up_weight.shape, jnp.bfloat16),
            pltpu.VMEM((n_inst, block, half + local), jnp.bfloat16),
            pltpu.VMEM((n_inst, block, half), jnp.bfloat16),
            pltpu.VMEM((2, steps, requests, half), jnp.bfloat16),
            pltpu.VMEM((2, 1, requests), jnp.int32),
            pltpu.VMEM((n_tp, rows, local), jnp.float32),
            pltpu.VMEM((n_tp, rows, local), jnp.float32),
            pltpu.VMEM((rank, rows), jnp.float32),
            pltpu.VMEM((rank, rows), jnp.float32),
            pltpu.VMEM((2, rank, rows), jnp.float32),
            pltpu.VMEM((n_tp, rank, rows), jnp.float32),
            pltpu.VMEM((n_tp, rank, rows), jnp.float32),
            pltpu.VMEM((rows, HEAD), jnp.float32),
            pltpu.VMEM((rows, HEAD), jnp.float32),
            pltpu.SemaphoreType.DMA((4,)),
            pltpu.SemaphoreType.DMA((5,)),
            pltpu.SemaphoreType.DMA((2, n_inst)),
            pltpu.SemaphoreType.DMA((2, n_inst)),
            pltpu.SemaphoreType.DMA((2, n_inst)),
            pltpu.SemaphoreType.DMA((2, 2)),
            pltpu.SemaphoreType.DMA((2, 2)),
            pltpu.SemaphoreType.DMA((2, n_tp)),
            pltpu.SemaphoreType.DMA((n_tp,)),
            pltpu.SemaphoreType.DMA((n_tp,)),
            pltpu.SemaphoreType.DMA((n_tp,)),
            pltpu.SemaphoreType.DMA((n_tp,)),
            pltpu.SemaphoreType.DMA((n_tp,)),
        ],
        compiler_params=pltpu.CompilerParams(
            collective_id=0, has_side_effects=True, vmem_limit_bytes=60 * 1024 * 1024
        ),
        name="lora_keys",
    )(
        pool_rows,
        request_slot.reshape(1, requests),
        lengths.reshape(1, requests),
        jnp.asarray(np.concatenate([freqs, freqs]).reshape(1, HEAD)),
        hidden,
        key_matrix,
        down_weight,
        up_weight,
    )


def solution(mesh):
    placed = (
        P(None, ("groups", "inst"), "tp"),
        P("tp", None),
        P("inst", None, "tp"),
        P("inst", None, "tp"),
        P(("groups", "inst")),
        P("groups"),
        P(("groups", "inst")),
    )
    return jax.shard_map(
        on_device,
        mesh=mesh,
        in_specs=placed,
        out_specs=P(None, ("groups", "inst"), "tp"),
        check_vma=False,
    )
```

```python
import functools

import jax
import jax.numpy as jnp
import numpy as np
from jax import lax
from jax.experimental import pallas as pl
from jax.experimental.pallas import tpu as pltpu
from jax.sharding import PartitionSpec as P

HEAD = 128
ADAPTER_SCALE = 2.0
ROPE_THETA = 500000.0
MESH_ID = pl.DeviceIdType.MESH


def rope_freqs(head_size):
    pair = np.arange(head_size // 2, dtype=np.float64)
    base = ROPE_THETA ** (-2.0 * pair / head_size)
    wavelen = 2.0 * np.pi / base
    smooth = (8192.0 / wavelen - 1.0) / 3.0
    blended = (1.0 - smooth) * base / 8.0 + smooth * base
    scaled = np.where(wavelen > 8192.0, base / 8.0, blended)
    return np.where(wavelen < 2048.0, base, scaled).astype(np.float32)


def kernel(
    n_inst, n_tp, n_act, rank, pool_rows_hbm, slot_hbm, len_hbm, freq_hbm,
    hidden_hbm, key_hbm, down_hbm, up_hbm, out_ref,
    pool_rows, slot, length, freq, hidden, key, down_low, down_high, up, low_half, high_half, guest, guest_slot,
    part, keys_in, score, total_score, help_out, help_in, score_in, cos_tab, sin_tab,
    small_sem, load_sem, out_right_sem, out_left_sem, in_sem, guest_out_sem, guest_in_sem,
    help_out_sem, help_in_sem, key_out_sem, key_in_sem, sc_out_sem, sc_in_sem,
):
    me = lax.axis_index("inst")
    tp = lax.axis_index("tp")
    _, steps, requests, half = hidden.shape
    rows = steps * requests
    local = up.shape[2]
    pool_count = down_low.shape[0]
    last = n_inst - 1
    is_end = (me == 0) | (me == last)

    load_down = [
        pltpu.make_async_copy(
            down_hbm.at[:, :, pl.ds(h * half, half)], down, load_sem.at[5 * h]
        )
        for h, down in enumerate((down_low, down_high))
    ]
    load_up = pltpu.make_async_copy(up_hbm, up, load_sem.at[1])
    load_hidden = [
        pltpu.make_async_copy(
            hidden_hbm.at[:, :, pl.ds(h * half, half)], hidden.at[h], load_sem.at[2 + h]
        )
        for h in range(2)
    ]
    load_key = pltpu.make_async_copy(key_hbm, key, load_sem.at[4])
    load_small = [
        pltpu.make_async_copy(src, dst, small_sem.at[i])
        for i, (src, dst) in enumerate(
            ((pool_rows_hbm, pool_rows), (slot_hbm, slot), (len_hbm, length), (freq_hbm, freq))
        )
    ]
    for copy in load_small:
        copy.start()
    load_down[0].start()
    load_up.start()
    load_down[1].start()

    barrier = pltpu.get_barrier_semaphore()
    for shift in (1, n_inst - 1):
        pl.semaphore_signal(
            barrier, inc=1, device_id={"inst": lax.rem(me + shift, n_inst)}, device_id_type=MESH_ID
        )
    for shift in range(1, n_tp):
        pl.semaphore_signal(
            barrier, inc=1, device_id={"tp": lax.rem(tp + shift, n_tp)}, device_id_type=MESH_ID
        )

    ends = (
        (0, 0, 1, {"inst": lax.rem(me + 1, n_inst)}),
        (1, last, last - 1, {"inst": lax.rem(me + n_inst - 1, n_inst)}),
    )
    for e, end, helper, _ in ends:
        for here, there in ((end, helper), (helper, end)):

            @pl.when(me == here)
            def _():
                for shift in range(1, n_tp):
                    pl.semaphore_signal(
                        barrier, inc=1, device_id={"inst": there, "tp": lax.rem(tp + shift, n_tp)},
                        device_id_type=MESH_ID,
                    )

    for copy in load_small:
        copy.wait()
    own_rows = [lax.rem(pool_rows[me * n_act + k], pool_count) for k in range(n_act)]
    load_down[0].wait()
    load_up.wait()
    for k, row in enumerate(own_rows):
        ranks = slice(k * rank, (k + 1) * rank)
        low_half[me, ranks, :half] = down_low[row]
        low_half[me, ranks, half:] = up[row]

    pairs = 0
    for _, end, helper, _ in ends:
        for here in (end, helper):
            pairs += jnp.where(me == here, 1, 0)
    pl.semaphore_wait(barrier, 2 + (n_tp - 1) * (1 + pairs))

    right = {"inst": lax.rem(me + 1, n_inst)}
    left = {"inst": lax.rem(me + n_inst - 1, n_inst)}

    def remote(src, dst, send_sem, recv_sem, device):
        return pltpu.make_async_remote_copy(
            src_ref=src, dst_ref=dst, send_sem=send_sem, recv_sem=recv_sem,
            device_id=device, device_id_type=MESH_ID,
        )

    def hop(h, owner, sems, device):
        buffer = high_half if h else low_half
        return remote(
            buffer.at[owner], buffer.at[owner], sems.at[h, owner], in_sem.at[h, owner], device
        )

    def go_right(h, owner):
        @pl.when(me + 1 < (last if h else n_inst))
        def _():
            hop(h, owner, out_right_sem, right).start()

    def go_left(h, owner):
        @pl.when(me > (1 if h else 0))
        def _():
            hop(h, owner, out_left_sem, left).start()

    def arrive(h, owner):
        hop(h, owner, out_right_sem, right).wait_recv()

    go_right(0, me)
    go_left(0, me)

    load_down[1].wait()
    for copy in load_hidden:
        copy.start()
    load_key.start()
    for k, row in enumerate(own_rows):
        high_half[me, k * rank : (k + 1) * rank, :] = down_high[row]

    for copy in load_hidden:
        copy.wait()
    load_key.wait()

    def send_keys(shift):
        return remote(
            part.at[shift], keys_in.at[shift], key_out_sem.at[shift], key_in_sem.at[shift],
            {"tp": lax.rem(tp + shift, n_tp)},
        )

    def partial_keys(shift):
        peer = lax.rem(tp + shift, n_tp)
        columns = pl.ds(pl.multiple_of(peer * local, local), local)
        part[shift] = jnp.dot(
            hidden[0].reshape(rows, half), key[:half, columns], preferred_element_type=jnp.float32
        ) + jnp.dot(
            hidden[1].reshape(rows, half), key[half:, columns], preferred_element_type=jnp.float32
        )

    for shift in range(1, n_tp):
        partial_keys(shift)
        send_keys(shift).start()
    partial_keys(0)

    slots = jnp.concatenate([slot[...]] * steps, axis=1)

    def pick(total, weights, values, wanted, owner):
        piece = lax.dot_general(
            weights, values, (((1,), (1,)), ((), ())), preferred_element_type=jnp.float32
        )
        for k in range(n_act):
            total += jnp.where(
                wanted == owner * n_act + k, piece[k * rank : (k + 1) * rank, :], 0.0
            )
        return total

    def add_low(owner):
        score[...] = pick(
            score[...], low_half[owner, :, :half], hidden[0].reshape(rows, half), slots, owner
        )

    def add_high(owner):
        score[...] = pick(
            score[...], high_half[owner], hidden[1].reshape(rows, half), slots, owner
        )

    score[...] = jnp.zeros((rank, rows), jnp.float32)
    add_low(me)
    add_high(me)

    lens = jnp.broadcast_to(length[...].astype(jnp.float32), (HEAD, requests)).T
    lane = lax.broadcasted_iota(jnp.int32, (requests, HEAD), 1)
    for s in range(steps):
        angle = (lens + float(s)) * freq[...]
        sine = jnp.sin(angle)
        cos_tab[s * requests : (s + 1) * requests, :] = jnp.cos(angle)
        sin_tab[s * requests : (s + 1) * requests, :] = jnp.where(lane < HEAD // 2, -sine, sine)

    @pl.when(me < last)
    def _():
        hop(0, me, out_right_sem, right).wait_send()

    go_right(1, me)

    @pl.when(me > 0)
    def _():
        hop(0, me, out_left_sem, left).wait_send()

    go_left(1, me)

    def send_guest(e, device):
        return (
            remote(hidden.at[1], guest.at[e], guest_out_sem.at[e, 0], guest_in_sem.at[e, 0], device),
            remote(slot, guest_slot.at[e], guest_out_sem.at[e, 1], guest_in_sem.at[e, 1], device),
        )

    for e, end, _, device in ends:
        sems = out_left_sem if e else out_right_sem

        @pl.when(me == end)
        def _():
            if n_inst > 2:
                hop(1, me, sems, device).wait_send()
            for copy in send_guest(e, device):
                copy.start()

    def add_guest(e, owner, total):
        wanted = jnp.concatenate([guest_slot[e]] * steps, axis=1)
        return pick(total, high_half[owner], guest[e].reshape(rows, half), wanted, owner)

    def step(d, carry):
        lower = me - d
        upper = me + d
        sides = ((lower, lower >= 0, go_right), (upper, upper < n_inst, go_left))
        for owner, there, go_on in sides:

            @pl.when(there)
            def _():
                arrive(0, owner)
                go_on(0, owner)

        for owner, there, go_on in sides:

            @pl.when(there)
            def _():
                add_low(owner)

        for e, end, helper, device in ends:

            @pl.when((me == helper) & (d == max(n_inst - 2, 1)))
            def _():
                for copy in send_guest(e, device):
                    copy.wait_recv()
                help_out[e] = lax.fori_loop(
                    1, n_inst - 1, functools.partial(add_guest, e),
                    jnp.zeros((rank, rows), jnp.float32),
                )

        for owner, there, go_on in sides:

            @pl.when(there & jnp.logical_not(is_end))
            def _():
                arrive(1, owner)
                go_on(1, owner)
                add_high(owner)

        return carry

    lax.fori_loop(1, n_inst, step, 0)

    def send_help(e, shift):
        return remote(
            help_out.at[e], help_in.at[shift], help_out_sem.at[e, shift], help_in_sem.at[shift],
            {"inst": ends[e][1], "tp": lax.rem(tp + shift, n_tp)},
        )

    for e, end, helper, device in ends:

        @pl.when(me == helper)
        def _():
            help_out[e] = add_guest(e, 0 if e else last, help_out[e])
            for shift in range(n_tp):
                send_help(e, shift).start()

    def send_score(shift):
        return remote(
            score, score_in.at[shift], sc_out_sem.at[shift], sc_in_sem.at[shift],
            {"tp": lax.rem(tp + shift, n_tp)},
        )

    for shift in range(1, n_tp):
        send_score(shift).start()

    for shift in range(1, n_tp):
        send_keys(shift).wait_recv()
        part[0] += keys_in[shift]

    for shift in range(1, n_tp):
        send_score(shift).wait_recv()
    shrink = score[...]
    for shift in range(1, n_tp):
        shrink += score_in[shift]
    total_score[...] = shrink

    @pl.when(is_end)
    def _():
        for shift in range(n_tp):
            send_help(0, shift).wait_recv()
            total_score[...] += help_in[shift]

    shrink = total_score[...].astype(jnp.bfloat16).astype(jnp.float32)

    def add_update(owner, total):
        spread = jnp.concatenate(
            [jnp.where(slots == owner * n_act + k, shrink, 0.0) for k in range(n_act)], axis=0
        )
        return total + lax.dot_general(
            spread.astype(jnp.bfloat16), low_half[owner, :, half:],
            (((0,), (0,)), ((), ())), preferred_element_type=jnp.float32,
        )

    update = lax.fori_loop(0, n_inst, add_update, jnp.zeros((rows, local), jnp.float32), unroll=n_inst <= 4)
    mixed = part[0] + ADAPTER_SCALE * update.astype(jnp.bfloat16).astype(jnp.float32)
    for h in range(local // HEAD):
        values = mixed[:, h * HEAD : (h + 1) * HEAD]
        turned = values * cos_tab[...] + pltpu.roll(values, HEAD // 2, 1) * sin_tab[...]
        out_ref[:, :, h * HEAD : (h + 1) * HEAD] = turned.astype(jnp.bfloat16).reshape(
            steps, requests, HEAD
        )

    for shift in range(1, n_tp):
        send_keys(shift).wait_send()
        send_score(shift).wait_send()
    for e, end, helper, device in ends:

        @pl.when(me == end)
        def _():
            for copy in send_guest(e, device):
                copy.wait_send()

        @pl.when(me == helper)
        def _():
            for shift in range(n_tp):
                send_help(e, shift).wait_send()

    def drain(owner, carry):
        @pl.when((owner < me) & (me < last))
        def _():
            hop(0, owner, out_right_sem, right).wait_send()

        @pl.when((owner > me) & (me > 0))
        def _():
            hop(0, owner, out_left_sem, left).wait_send()

        @pl.when((owner <= me) & (me + 1 < last) & (me > 0))
        def _():
            hop(1, owner, out_right_sem, right).wait_send()

        @pl.when((owner >= me) & (me > 1) & (me < last))
        def _():
            hop(1, owner, out_left_sem, left).wait_send()

        return carry

    lax.fori_loop(0, n_inst, drain, 0)


def on_device(
    hidden, key_matrix, down_weight, up_weight, request_slot, pool_rows, lengths
):
    n_inst = lax.axis_size("inst")
    n_tp = lax.axis_size("tp")
    steps, requests, width = hidden.shape
    _, rank, local = up_weight.shape
    n_act = pool_rows.shape[0] // n_inst
    rows = steps * requests
    block = n_act * rank
    freqs = rope_freqs(HEAD)
    half = width // 2
    vmem = pl.BlockSpec(memory_space=pltpu.VMEM)
    hbm = pl.BlockSpec(memory_space=pltpu.HBM)
    return pl.pallas_call(
        functools.partial(kernel, n_inst, n_tp, n_act, rank),
        out_shape=jax.ShapeDtypeStruct((steps, requests, local), jnp.bfloat16),
        in_specs=[hbm] * 8,
        out_specs=vmem,
        scratch_shapes=[
            pltpu.SMEM(pool_rows.shape, jnp.int32),
            pltpu.VMEM((1, requests), jnp.int32),
            pltpu.VMEM((1, requests), jnp.int32),
            pltpu.VMEM((1, HEAD), jnp.float32),
            pltpu.VMEM((2, steps, requests, half), jnp.bfloat16),
            pltpu.VMEM(key_matrix.shape, jnp.bfloat16),
            pltpu.VMEM((*down_weight.shape[:2], half), jnp.bfloat16),
            pltpu.VMEM((*down_weight.shape[:2], half), jnp.bfloat16),
            pltpu.VMEM(up_weight.shape, jnp.bfloat16),
            pltpu.VMEM((n_inst, block, half + local), jnp.bfloat16),
            pltpu.VMEM((n_inst, block, half), jnp.bfloat16),
            pltpu.VMEM((2, steps, requests, half), jnp.bfloat16),
            pltpu.VMEM((2, 1, requests), jnp.int32),
            pltpu.VMEM((n_tp, rows, local), jnp.float32),
            pltpu.VMEM((n_tp, rows, local), jnp.float32),
            pltpu.VMEM((rank, rows), jnp.float32),
            pltpu.VMEM((rank, rows), jnp.float32),
            pltpu.VMEM((2, rank, rows), jnp.float32),
            pltpu.VMEM((n_tp, rank, rows), jnp.float32),
            pltpu.VMEM((n_tp, rank, rows), jnp.float32),
            pltpu.VMEM((rows, HEAD), jnp.float32),
            pltpu.VMEM((rows, HEAD), jnp.float32),
            pltpu.SemaphoreType.DMA((4,)),
            pltpu.SemaphoreType.DMA((6,)),
            pltpu.SemaphoreType.DMA((2, n_inst)),
            pltpu.SemaphoreType.DMA((2, n_inst)),
            pltpu.SemaphoreType.DMA((2, n_inst)),
            pltpu.SemaphoreType.DMA((2, 2)),
            pltpu.SemaphoreType.DMA((2, 2)),
            pltpu.SemaphoreType.DMA((2, n_tp)),
            pltpu.SemaphoreType.DMA((n_tp,)),
            pltpu.SemaphoreType.DMA((n_tp,)),
            pltpu.SemaphoreType.DMA((n_tp,)),
            pltpu.SemaphoreType.DMA((n_tp,)),
            pltpu.SemaphoreType.DMA((n_tp,)),
        ],
        compiler_params=pltpu.CompilerParams(
            collective_id=0, has_side_effects=True, vmem_limit_bytes=60 * 1024 * 1024
        ),
        name="lora_keys",
    )(
        pool_rows,
        request_slot.reshape(1, requests),
        lengths.reshape(1, requests),
        jnp.asarray(np.concatenate([freqs, freqs]).reshape(1, HEAD)),
        hidden,
        key_matrix,
        down_weight,
        up_weight,
    )


def solution(mesh):
    placed = (
        P(None, ("groups", "inst"), "tp"),
        P("tp", None),
        P("inst", None, "tp"),
        P("inst", None, "tp"),
        P(("groups", "inst")),
        P("groups"),
        P(("groups", "inst")),
    )
    return jax.shard_map(
        on_device,
        mesh=mesh,
        in_specs=placed,
        out_specs=P(None, ("groups", "inst"), "tp"),
        check_vma=False,
    )
```

```python
import functools

import jax
import jax.numpy as jnp
import numpy as np
from jax import lax
from jax.experimental import pallas as pl
from jax.experimental.pallas import tpu as pltpu
from jax.sharding import PartitionSpec as P

HEAD = 128
ADAPTER_SCALE = 2.0
ROPE_THETA = 500000.0
MESH_ID = pl.DeviceIdType.MESH


def rope_freqs(head_size):
    pair = np.arange(head_size // 2, dtype=np.float64)
    base = ROPE_THETA ** (-2.0 * pair / head_size)
    wavelen = 2.0 * np.pi / base
    smooth = (8192.0 / wavelen - 1.0) / 3.0
    blended = (1.0 - smooth) * base / 8.0 + smooth * base
    scaled = np.where(wavelen > 8192.0, base / 8.0, blended)
    return np.where(wavelen < 2048.0, base, scaled).astype(np.float32)


def kernel(
    n_inst, n_tp, n_act, rank, pool_rows_hbm, slot_hbm, len_hbm, freq_hbm,
    hidden_hbm, key_hbm, down_hbm, up_hbm, out_ref,
    pool_rows, slot, length, freq, hidden, key, down_low, down_high, up, low_half, high_half, guest, guest_slot,
    part, keys_in, score, total_score, help_out, help_in, score_in, cos_tab, sin_tab,
    small_sem, load_sem, out_right_sem, out_left_sem, in_sem, guest_out_sem, guest_in_sem,
    help_out_sem, help_in_sem, key_out_sem, key_in_sem, sc_out_sem, sc_in_sem,
):
    me = lax.axis_index("inst")
    tp = lax.axis_index("tp")
    _, steps, requests, half = hidden.shape
    rows = steps * requests
    local = up.shape[2]
    pool_count = down_low.shape[0]
    last = n_inst - 1
    is_end = (me == 0) | (me == last)

    load_down = [
        pltpu.make_async_copy(
            down_hbm.at[:, :, pl.ds(h * half, half)], down, load_sem.at[5 * h]
        )
        for h, down in enumerate((down_low, down_high))
    ]
    load_up = pltpu.make_async_copy(up_hbm, up, load_sem.at[1])
    load_hidden = [
        pltpu.make_async_copy(
            hidden_hbm.at[:, :, pl.ds(h * half, half)], hidden.at[h], load_sem.at[2 + h]
        )
        for h in range(2)
    ]
    load_key = pltpu.make_async_copy(key_hbm, key, load_sem.at[4])
    load_small = [
        pltpu.make_async_copy(src, dst, small_sem.at[i])
        for i, (src, dst) in enumerate(
            ((pool_rows_hbm, pool_rows), (slot_hbm, slot), (len_hbm, length), (freq_hbm, freq))
        )
    ]
    for copy in load_small:
        copy.start()
    load_down[0].start()
    load_up.start()
    load_down[1].start()

    barrier = pltpu.get_barrier_semaphore()
    for shift in (1, n_inst - 1):
        pl.semaphore_signal(
            barrier, inc=1, device_id={"inst": lax.rem(me + shift, n_inst)}, device_id_type=MESH_ID
        )
    for shift in range(1, n_tp):
        pl.semaphore_signal(
            barrier, inc=1, device_id={"tp": lax.rem(tp + shift, n_tp)}, device_id_type=MESH_ID
        )

    ends = (
        (0, 0, 1, {"inst": lax.rem(me + 1, n_inst)}),
        (1, last, last - 1, {"inst": lax.rem(me + n_inst - 1, n_inst)}),
    )
    for e, end, helper, _ in ends:
        for here, there in ((end, helper), (helper, end)):

            @pl.when(me == here)
            def _():
                for shift in range(1, n_tp):
                    pl.semaphore_signal(
                        barrier, inc=1, device_id={"inst": there, "tp": lax.rem(tp + shift, n_tp)},
                        device_id_type=MESH_ID,
                    )

    for copy in load_small:
        copy.wait()
    own_rows = [lax.rem(pool_rows[me * n_act + k], pool_count) for k in range(n_act)]
    load_down[0].wait()
    load_up.wait()
    for k, row in enumerate(own_rows):
        ranks = slice(k * rank, (k + 1) * rank)
        low_half[me, ranks, :half] = down_low[row]
        low_half[me, ranks, half:] = up[row]

    pairs = 0
    for _, end, helper, _ in ends:
        for here in (end, helper):
            pairs += jnp.where(me == here, 1, 0)
    pl.semaphore_wait(barrier, 2 + (n_tp - 1) * (1 + pairs))

    right = {"inst": lax.rem(me + 1, n_inst)}
    left = {"inst": lax.rem(me + n_inst - 1, n_inst)}

    def remote(src, dst, send_sem, recv_sem, device):
        return pltpu.make_async_remote_copy(
            src_ref=src, dst_ref=dst, send_sem=send_sem, recv_sem=recv_sem,
            device_id=device, device_id_type=MESH_ID,
        )

    def hop(h, owner, sems, device):
        buffer = high_half if h else low_half
        return remote(
            buffer.at[owner], buffer.at[owner], sems.at[h, owner], in_sem.at[h, owner], device
        )

    def go_right(h, owner):
        @pl.when(me + 1 < (last if h else n_inst))
        def _():
            hop(h, owner, out_right_sem, right).start()

    def go_left(h, owner):
        @pl.when(me > (1 if h else 0))
        def _():
            hop(h, owner, out_left_sem, left).start()

    def arrive(h, owner):
        hop(h, owner, out_right_sem, right).wait_recv()

    go_right(0, me)
    go_left(0, me)

    load_down[1].wait()
    for copy in load_hidden:
        copy.start()
    load_key.start()
    for k, row in enumerate(own_rows):
        high_half[me, k * rank : (k + 1) * rank, :] = down_high[row]

    for copy in load_hidden:
        copy.wait()
    load_key.wait()

    def send_keys(shift):
        return remote(
            part.at[shift], keys_in.at[shift], key_out_sem.at[shift], key_in_sem.at[shift],
            {"tp": lax.rem(tp + shift, n_tp)},
        )

    def partial_keys(shift):
        peer = lax.rem(tp + shift, n_tp)
        columns = pl.ds(pl.multiple_of(peer * local, local), local)
        part[shift] = jnp.dot(
            hidden[0].reshape(rows, half), key[:half, columns], preferred_element_type=jnp.float32
        ) + jnp.dot(
            hidden[1].reshape(rows, half), key[half:, columns], preferred_element_type=jnp.float32
        )

    for shift in range(1, n_tp):
        partial_keys(shift)
        send_keys(shift).start()
    partial_keys(0)

    slots = jnp.concatenate([slot[...]] * steps, axis=1)

    def pick(total, weights, values, wanted, owner):
        piece = lax.dot_general(
            weights, values, (((1,), (1,)), ((), ())), preferred_element_type=jnp.float32
        )
        for k in range(n_act):
            total += jnp.where(
                wanted == owner * n_act + k, piece[k * rank : (k + 1) * rank, :], 0.0
            )
        return total

    def add_low(owner):
        score[...] = pick(
            score[...], low_half[owner, :, :half], hidden[0].reshape(rows, half), slots, owner
        )

    def add_high(owner):
        score[...] = pick(
            score[...], high_half[owner], hidden[1].reshape(rows, half), slots, owner
        )

    score[...] = jnp.zeros((rank, rows), jnp.float32)
    add_low(me)
    add_high(me)

    @pl.when(me < last)
    def _():
        hop(0, me, out_right_sem, right).wait_send()

    go_right(1, me)

    @pl.when(me > 0)
    def _():
        hop(0, me, out_left_sem, left).wait_send()

    go_left(1, me)

    def send_guest(e, device):
        return (
            remote(hidden.at[1], guest.at[e], guest_out_sem.at[e, 0], guest_in_sem.at[e, 0], device),
            remote(slot, guest_slot.at[e], guest_out_sem.at[e, 1], guest_in_sem.at[e, 1], device),
        )

    for e, end, _, device in ends:
        sems = out_left_sem if e else out_right_sem

        @pl.when(me == end)
        def _():
            if n_inst > 2:
                hop(1, me, sems, device).wait_send()
            for copy in send_guest(e, device):
                copy.start()

    def add_guest(e, owner, total):
        wanted = jnp.concatenate([guest_slot[e]] * steps, axis=1)
        return pick(total, high_half[owner], guest[e].reshape(rows, half), wanted, owner)

    def make_tables():
        lens = jnp.broadcast_to(length[...].astype(jnp.float32), (HEAD, requests)).T
        lane = lax.broadcasted_iota(jnp.int32, (requests, HEAD), 1)
        for s in range(steps):
            angle = (lens + float(s)) * freq[...]
            sine = jnp.sin(angle)
            cos_tab[s * requests : (s + 1) * requests, :] = jnp.cos(angle)
            sin_tab[s * requests : (s + 1) * requests, :] = jnp.where(lane < HEAD // 2, -sine, sine)

    def step(d, carry):
        lower = me - d
        upper = me + d
        sides = ((lower, lower >= 0, go_right), (upper, upper < n_inst, go_left))
        for owner, there, go_on in sides:

            @pl.when(there)
            def _():
                arrive(0, owner)
                go_on(0, owner)

        for owner, there, go_on in sides:

            @pl.when(there)
            def _():
                add_low(owner)

        pl.when(d == 1)(make_tables)

        for e, end, helper, device in ends:

            @pl.when((me == helper) & (d == max(n_inst - 2, 1)))
            def _():
                for copy in send_guest(e, device):
                    copy.wait_recv()
                help_out[e] = lax.fori_loop(
                    1, n_inst - 1, functools.partial(add_guest, e),
                    jnp.zeros((rank, rows), jnp.float32),
                )

        for owner, there, go_on in sides:

            @pl.when(there & jnp.logical_not(is_end))
            def _():
                arrive(1, owner)
                go_on(1, owner)
                add_high(owner)

        return carry

    lax.fori_loop(1, n_inst, step, 0)

    def send_help(e, shift):
        return remote(
            help_out.at[e], help_in.at[shift], help_out_sem.at[e, shift], help_in_sem.at[shift],
            {"inst": ends[e][1], "tp": lax.rem(tp + shift, n_tp)},
        )

    for e, end, helper, device in ends:

        @pl.when(me == helper)
        def _():
            help_out[e] = add_guest(e, 0 if e else last, help_out[e])
            for shift in range(n_tp):
                send_help(e, shift).start()

    def send_score(shift):
        return remote(
            score, score_in.at[shift], sc_out_sem.at[shift], sc_in_sem.at[shift],
            {"tp": lax.rem(tp + shift, n_tp)},
        )

    for shift in range(1, n_tp):
        send_score(shift).start()

    for shift in range(1, n_tp):
        send_keys(shift).wait_recv()
        part[0] += keys_in[shift]

    for shift in range(1, n_tp):
        send_score(shift).wait_recv()
    shrink = score[...]
    for shift in range(1, n_tp):
        shrink += score_in[shift]
    total_score[...] = shrink

    @pl.when(is_end)
    def _():
        for shift in range(n_tp):
            send_help(0, shift).wait_recv()
            total_score[...] += help_in[shift]

    shrink = total_score[...].astype(jnp.bfloat16).astype(jnp.float32)

    def add_update(owner, total):
        spread = jnp.concatenate(
            [jnp.where(slots == owner * n_act + k, shrink, 0.0) for k in range(n_act)], axis=0
        )
        return total + lax.dot_general(
            spread.astype(jnp.bfloat16), low_half[owner, :, half:],
            (((0,), (0,)), ((), ())), preferred_element_type=jnp.float32,
        )

    update = lax.fori_loop(0, n_inst, add_update, jnp.zeros((rows, local), jnp.float32), unroll=n_inst <= 4)
    mixed = part[0] + ADAPTER_SCALE * update.astype(jnp.bfloat16).astype(jnp.float32)
    for h in range(local // HEAD):
        values = mixed[:, h * HEAD : (h + 1) * HEAD]
        turned = values * cos_tab[...] + pltpu.roll(values, HEAD // 2, 1) * sin_tab[...]
        out_ref[:, :, h * HEAD : (h + 1) * HEAD] = turned.astype(jnp.bfloat16).reshape(
            steps, requests, HEAD
        )

    for shift in range(1, n_tp):
        send_keys(shift).wait_send()
        send_score(shift).wait_send()
    for e, end, helper, device in ends:

        @pl.when(me == end)
        def _():
            for copy in send_guest(e, device):
                copy.wait_send()

        @pl.when(me == helper)
        def _():
            for shift in range(n_tp):
                send_help(e, shift).wait_send()

    def drain(owner, carry):
        @pl.when((owner < me) & (me < last))
        def _():
            hop(0, owner, out_right_sem, right).wait_send()

        @pl.when((owner > me) & (me > 0))
        def _():
            hop(0, owner, out_left_sem, left).wait_send()

        @pl.when((owner <= me) & (me + 1 < last) & (me > 0))
        def _():
            hop(1, owner, out_right_sem, right).wait_send()

        @pl.when((owner >= me) & (me > 1) & (me < last))
        def _():
            hop(1, owner, out_left_sem, left).wait_send()

        return carry

    lax.fori_loop(0, n_inst, drain, 0)


def on_device(
    hidden, key_matrix, down_weight, up_weight, request_slot, pool_rows, lengths
):
    n_inst = lax.axis_size("inst")
    n_tp = lax.axis_size("tp")
    steps, requests, width = hidden.shape
    _, rank, local = up_weight.shape
    n_act = pool_rows.shape[0] // n_inst
    rows = steps * requests
    block = n_act * rank
    freqs = rope_freqs(HEAD)
    half = width // 2
    vmem = pl.BlockSpec(memory_space=pltpu.VMEM)
    hbm = pl.BlockSpec(memory_space=pltpu.HBM)
    return pl.pallas_call(
        functools.partial(kernel, n_inst, n_tp, n_act, rank),
        out_shape=jax.ShapeDtypeStruct((steps, requests, local), jnp.bfloat16),
        in_specs=[hbm] * 8,
        out_specs=vmem,
        scratch_shapes=[
            pltpu.SMEM(pool_rows.shape, jnp.int32),
            pltpu.VMEM((1, requests), jnp.int32),
            pltpu.VMEM((1, requests), jnp.int32),
            pltpu.VMEM((1, HEAD), jnp.float32),
            pltpu.VMEM((2, steps, requests, half), jnp.bfloat16),
            pltpu.VMEM(key_matrix.shape, jnp.bfloat16),
            pltpu.VMEM((*down_weight.shape[:2], half), jnp.bfloat16),
            pltpu.VMEM((*down_weight.shape[:2], half), jnp.bfloat16),
            pltpu.VMEM(up_weight.shape, jnp.bfloat16),
            pltpu.VMEM((n_inst, block, half + local), jnp.bfloat16),
            pltpu.VMEM((n_inst, block, half), jnp.bfloat16),
            pltpu.VMEM((2, steps, requests, half), jnp.bfloat16),
            pltpu.VMEM((2, 1, requests), jnp.int32),
            pltpu.VMEM((n_tp, rows, local), jnp.float32),
            pltpu.VMEM((n_tp, rows, local), jnp.float32),
            pltpu.VMEM((rank, rows), jnp.float32),
            pltpu.VMEM((rank, rows), jnp.float32),
            pltpu.VMEM((2, rank, rows), jnp.float32),
            pltpu.VMEM((n_tp, rank, rows), jnp.float32),
            pltpu.VMEM((n_tp, rank, rows), jnp.float32),
            pltpu.VMEM((rows, HEAD), jnp.float32),
            pltpu.VMEM((rows, HEAD), jnp.float32),
            pltpu.SemaphoreType.DMA((4,)),
            pltpu.SemaphoreType.DMA((6,)),
            pltpu.SemaphoreType.DMA((2, n_inst)),
            pltpu.SemaphoreType.DMA((2, n_inst)),
            pltpu.SemaphoreType.DMA((2, n_inst)),
            pltpu.SemaphoreType.DMA((2, 2)),
            pltpu.SemaphoreType.DMA((2, 2)),
            pltpu.SemaphoreType.DMA((2, n_tp)),
            pltpu.SemaphoreType.DMA((n_tp,)),
            pltpu.SemaphoreType.DMA((n_tp,)),
            pltpu.SemaphoreType.DMA((n_tp,)),
            pltpu.SemaphoreType.DMA((n_tp,)),
            pltpu.SemaphoreType.DMA((n_tp,)),
        ],
        compiler_params=pltpu.CompilerParams(
            collective_id=0, has_side_effects=True, vmem_limit_bytes=60 * 1024 * 1024
        ),
        name="lora_keys",
    )(
        pool_rows,
        request_slot.reshape(1, requests),
        lengths.reshape(1, requests),
        jnp.asarray(np.concatenate([freqs, freqs]).reshape(1, HEAD)),
        hidden,
        key_matrix,
        down_weight,
        up_weight,
    )


def solution(mesh):
    placed = (
        P(None, ("groups", "inst"), "tp"),
        P("tp", None),
        P("inst", None, "tp"),
        P("inst", None, "tp"),
        P(("groups", "inst")),
        P("groups"),
        P(("groups", "inst")),
    )
    return jax.shard_map(
        on_device,
        mesh=mesh,
        in_specs=placed,
        out_specs=P(None, ("groups", "inst"), "tp"),
        check_vma=False,
    )
```

```python
import functools

import jax
import jax.numpy as jnp
import numpy as np
from jax import lax
from jax.experimental import pallas as pl
from jax.experimental.pallas import tpu as pltpu
from jax.sharding import PartitionSpec as P

HEAD = 128
ADAPTER_SCALE = 2.0
ROPE_THETA = 500000.0
MESH_ID = pl.DeviceIdType.MESH


def rope_freqs(head_size):
    pair = np.arange(head_size // 2, dtype=np.float64)
    base = ROPE_THETA ** (-2.0 * pair / head_size)
    wavelen = 2.0 * np.pi / base
    smooth = (8192.0 / wavelen - 1.0) / 3.0
    blended = (1.0 - smooth) * base / 8.0 + smooth * base
    scaled = np.where(wavelen > 8192.0, base / 8.0, blended)
    return np.where(wavelen < 2048.0, base, scaled).astype(np.float32)


def kernel(
    n_inst, n_tp, n_act, rank, pool_rows_hbm, slot_hbm, len_hbm, freq_hbm,
    hidden_hbm, key_hbm, down_hbm, up_hbm, out_ref,
    pool_rows, slot, length, freq, hidden, key, down_low, down_high, up, low_half, high_half, guest, guest_slot,
    part, keys_in, score, total_score, help_out, help_in, score_in, cos_tab, sin_tab,
    small_sem, load_sem, out_right_sem, out_left_sem, in_sem, guest_out_sem, guest_in_sem,
    help_out_sem, help_in_sem, key_out_sem, key_in_sem, sc_out_sem, sc_in_sem,
):
    me = lax.axis_index("inst")
    tp = lax.axis_index("tp")
    _, steps, requests, half = hidden.shape
    rows = steps * requests
    local = up.shape[2]
    pool_count = down_low.shape[0]
    last = n_inst - 1
    is_end = (me == 0) | (me == last)

    load_down = [
        pltpu.make_async_copy(
            down_hbm.at[:, :, pl.ds(h * half, half)], down, load_sem.at[5 * h]
        )
        for h, down in enumerate((down_low, down_high))
    ]
    load_up = pltpu.make_async_copy(up_hbm, up, load_sem.at[1])
    load_hidden = [
        pltpu.make_async_copy(
            hidden_hbm.at[:, :, pl.ds(h * half, half)], hidden.at[h], load_sem.at[2 + h]
        )
        for h in range(2)
    ]
    load_key = pltpu.make_async_copy(key_hbm, key, load_sem.at[4])
    load_small = [
        pltpu.make_async_copy(src, dst, small_sem.at[i])
        for i, (src, dst) in enumerate(
            ((pool_rows_hbm, pool_rows), (slot_hbm, slot), (len_hbm, length), (freq_hbm, freq))
        )
    ]
    for copy in load_small:
        copy.start()
    load_down[0].start()
    load_up.start()
    load_down[1].start()

    barrier = pltpu.get_barrier_semaphore()
    for shift in (1, n_inst - 1):
        pl.semaphore_signal(
            barrier, inc=1, device_id={"inst": lax.rem(me + shift, n_inst)}, device_id_type=MESH_ID
        )
    for shift in range(1, n_tp):
        pl.semaphore_signal(
            barrier, inc=1, device_id={"tp": lax.rem(tp + shift, n_tp)}, device_id_type=MESH_ID
        )

    ends = (
        (0, 0, 1, {"inst": lax.rem(me + 1, n_inst)}),
        (1, last, last - 1, {"inst": lax.rem(me + n_inst - 1, n_inst)}),
    )
    for e, end, helper, _ in ends:
        for here, there in ((end, helper), (helper, end)):

            @pl.when(me == here)
            def _():
                for shift in range(1, n_tp):
                    pl.semaphore_signal(
                        barrier, inc=1, device_id={"inst": there, "tp": lax.rem(tp + shift, n_tp)},
                        device_id_type=MESH_ID,
                    )

    for copy in load_small:
        copy.wait()
    own_rows = [lax.rem(pool_rows[me * n_act + k], pool_count) for k in range(n_act)]
    load_down[0].wait()
    load_up.wait()
    for k, row in enumerate(own_rows):
        ranks = slice(k * rank, (k + 1) * rank)
        low_half[me, ranks, :half] = down_low[row]
        low_half[me, ranks, half:] = up[row]

    pairs = 0
    for _, end, helper, _ in ends:
        for here in (end, helper):
            pairs += jnp.where(me == here, 1, 0)
    pl.semaphore_wait(barrier, 2 + (n_tp - 1) * (1 + pairs))

    right = {"inst": lax.rem(me + 1, n_inst)}
    left = {"inst": lax.rem(me + n_inst - 1, n_inst)}

    def remote(src, dst, send_sem, recv_sem, device):
        return pltpu.make_async_remote_copy(
            src_ref=src, dst_ref=dst, send_sem=send_sem, recv_sem=recv_sem,
            device_id=device, device_id_type=MESH_ID,
        )

    def hop(h, owner, sems, device):
        buffer = high_half if h else low_half
        return remote(
            buffer.at[owner], buffer.at[owner], sems.at[h, owner], in_sem.at[h, owner], device
        )

    def go_right(h, owner):
        @pl.when(me + 1 < (last if h else n_inst))
        def _():
            hop(h, owner, out_right_sem, right).start()

    def go_left(h, owner):
        @pl.when(me > (1 if h else 0))
        def _():
            hop(h, owner, out_left_sem, left).start()

    def arrive(h, owner):
        hop(h, owner, out_right_sem, right).wait_recv()

    go_right(0, me)
    go_left(0, me)

    load_down[1].wait()
    for copy in load_hidden:
        copy.start()
    load_key.start()
    for k, row in enumerate(own_rows):
        high_half[me, k * rank : (k + 1) * rank, :] = down_high[row]
    go_right(1, me)
    go_left(1, me)

    for copy in load_hidden:
        copy.wait()
    load_key.wait()

    def send_keys(shift):
        return remote(
            part.at[shift], keys_in.at[shift], key_out_sem.at[shift], key_in_sem.at[shift],
            {"tp": lax.rem(tp + shift, n_tp)},
        )

    def partial_keys(shift):
        peer = lax.rem(tp + shift, n_tp)
        columns = pl.ds(pl.multiple_of(peer * local, local), local)
        part[shift] = jnp.dot(
            hidden[0].reshape(rows, half), key[:half, columns], preferred_element_type=jnp.float32
        ) + jnp.dot(
            hidden[1].reshape(rows, half), key[half:, columns], preferred_element_type=jnp.float32
        )

    for shift in range(1, n_tp):
        partial_keys(shift)
        send_keys(shift).start()
    partial_keys(0)

    slots = jnp.concatenate([slot[...]] * steps, axis=1)

    def pick(total, weights, values, wanted, owner):
        piece = lax.dot_general(
            weights, values, (((1,), (1,)), ((), ())), preferred_element_type=jnp.float32
        )
        for k in range(n_act):
            total += jnp.where(
                wanted == owner * n_act + k, piece[k * rank : (k + 1) * rank, :], 0.0
            )
        return total

    def add_low(owner):
        score[...] = pick(
            score[...], low_half[owner, :, :half], hidden[0].reshape(rows, half), slots, owner
        )

    def add_high(owner):
        score[...] = pick(
            score[...], high_half[owner], hidden[1].reshape(rows, half), slots, owner
        )

    score[...] = jnp.zeros((rank, rows), jnp.float32)
    add_low(me)
    add_high(me)

    def send_guest(e, device):
        return (
            remote(hidden.at[1], guest.at[e], guest_out_sem.at[e, 0], guest_in_sem.at[e, 0], device),
            remote(slot, guest_slot.at[e], guest_out_sem.at[e, 1], guest_in_sem.at[e, 1], device),
        )

    for e, end, _, device in ends:
        sems = out_left_sem if e else out_right_sem

        @pl.when(me == end)
        def _():
            if n_inst > 2:
                hop(1, me, sems, device).wait_send()
            for copy in send_guest(e, device):
                copy.start()

    def add_guest(e, owner, total):
        wanted = jnp.concatenate([guest_slot[e]] * steps, axis=1)
        return pick(total, high_half[owner], guest[e].reshape(rows, half), wanted, owner)

    def make_tables():
        lens = jnp.broadcast_to(length[...].astype(jnp.float32), (HEAD, requests)).T
        lane = lax.broadcasted_iota(jnp.int32, (requests, HEAD), 1)
        for s in range(steps):
            angle = (lens + float(s)) * freq[...]
            sine = jnp.sin(angle)
            cos_tab[s * requests : (s + 1) * requests, :] = jnp.cos(angle)
            sin_tab[s * requests : (s + 1) * requests, :] = jnp.where(lane < HEAD // 2, -sine, sine)

    def step(d, carry):
        lower = me - d
        upper = me + d
        sides = ((lower, lower >= 0, go_right), (upper, upper < n_inst, go_left))
        for owner, there, go_on in sides:

            @pl.when(there)
            def _():
                arrive(0, owner)
                go_on(0, owner)

        for owner, there, go_on in sides:

            @pl.when(there)
            def _():
                add_low(owner)

        pl.when(d == 1)(make_tables)

        for e, end, helper, device in ends:

            @pl.when((me == helper) & (d == max(n_inst - 2, 1)))
            def _():
                for copy in send_guest(e, device):
                    copy.wait_recv()
                help_out[e] = lax.fori_loop(
                    1, n_inst - 1, functools.partial(add_guest, e),
                    jnp.zeros((rank, rows), jnp.float32),
                )

        for owner, there, go_on in sides:

            @pl.when(there & jnp.logical_not(is_end))
            def _():
                arrive(1, owner)
                go_on(1, owner)
                add_high(owner)

        return carry

    lax.fori_loop(1, n_inst, step, 0)

    def send_help(e, shift):
        return remote(
            help_out.at[e], help_in.at[shift], help_out_sem.at[e, shift], help_in_sem.at[shift],
            {"inst": ends[e][1], "tp": lax.rem(tp + shift, n_tp)},
        )

    for e, end, helper, device in ends:

        @pl.when(me == helper)
        def _():
            help_out[e] = add_guest(e, 0 if e else last, help_out[e])
            for shift in range(n_tp):
                send_help(e, shift).start()

    def send_score(shift):
        return remote(
            score, score_in.at[shift], sc_out_sem.at[shift], sc_in_sem.at[shift],
            {"tp": lax.rem(tp + shift, n_tp)},
        )

    for shift in range(1, n_tp):
        send_score(shift).start()

    for shift in range(1, n_tp):
        send_keys(shift).wait_recv()
        part[0] += keys_in[shift]

    for shift in range(1, n_tp):
        send_score(shift).wait_recv()
    shrink = score[...]
    for shift in range(1, n_tp):
        shrink += score_in[shift]
    total_score[...] = shrink

    @pl.when(is_end)
    def _():
        for shift in range(n_tp):
            send_help(0, shift).wait_recv()
            total_score[...] += help_in[shift]

    shrink = total_score[...].astype(jnp.bfloat16).astype(jnp.float32)

    def add_update(owner, total):
        spread = jnp.concatenate(
            [jnp.where(slots == owner * n_act + k, shrink, 0.0) for k in range(n_act)], axis=0
        )
        return total + lax.dot_general(
            spread.astype(jnp.bfloat16), low_half[owner, :, half:],
            (((0,), (0,)), ((), ())), preferred_element_type=jnp.float32,
        )

    update = lax.fori_loop(0, n_inst, add_update, jnp.zeros((rows, local), jnp.float32), unroll=n_inst <= 4)
    mixed = part[0] + ADAPTER_SCALE * update.astype(jnp.bfloat16).astype(jnp.float32)
    for h in range(local // HEAD):
        values = mixed[:, h * HEAD : (h + 1) * HEAD]
        turned = values * cos_tab[...] + pltpu.roll(values, HEAD // 2, 1) * sin_tab[...]
        out_ref[:, :, h * HEAD : (h + 1) * HEAD] = turned.astype(jnp.bfloat16).reshape(
            steps, requests, HEAD
        )

    for shift in range(1, n_tp):
        send_keys(shift).wait_send()
        send_score(shift).wait_send()
    for e, end, helper, device in ends:

        @pl.when(me == end)
        def _():
            for copy in send_guest(e, device):
                copy.wait_send()

        @pl.when(me == helper)
        def _():
            for shift in range(n_tp):
                send_help(e, shift).wait_send()

    def drain(owner, carry):
        @pl.when((owner <= me) & (me < last))
        def _():
            hop(0, owner, out_right_sem, right).wait_send()

        @pl.when((owner >= me) & (me > 0))
        def _():
            hop(0, owner, out_left_sem, left).wait_send()

        @pl.when((owner <= me) & (me + 1 < last) & (me > 0))
        def _():
            hop(1, owner, out_right_sem, right).wait_send()

        @pl.when((owner >= me) & (me > 1) & (me < last))
        def _():
            hop(1, owner, out_left_sem, left).wait_send()

        return carry

    lax.fori_loop(0, n_inst, drain, 0)


def on_device(
    hidden, key_matrix, down_weight, up_weight, request_slot, pool_rows, lengths
):
    n_inst = lax.axis_size("inst")
    n_tp = lax.axis_size("tp")
    steps, requests, width = hidden.shape
    _, rank, local = up_weight.shape
    n_act = pool_rows.shape[0] // n_inst
    rows = steps * requests
    block = n_act * rank
    freqs = rope_freqs(HEAD)
    half = width // 2
    vmem = pl.BlockSpec(memory_space=pltpu.VMEM)
    hbm = pl.BlockSpec(memory_space=pltpu.HBM)
    return pl.pallas_call(
        functools.partial(kernel, n_inst, n_tp, n_act, rank),
        out_shape=jax.ShapeDtypeStruct((steps, requests, local), jnp.bfloat16),
        in_specs=[hbm] * 8,
        out_specs=vmem,
        scratch_shapes=[
            pltpu.SMEM(pool_rows.shape, jnp.int32),
            pltpu.VMEM((1, requests), jnp.int32),
            pltpu.VMEM((1, requests), jnp.int32),
            pltpu.VMEM((1, HEAD), jnp.float32),
            pltpu.VMEM((2, steps, requests, half), jnp.bfloat16),
            pltpu.VMEM(key_matrix.shape, jnp.bfloat16),
            pltpu.VMEM((*down_weight.shape[:2], half), jnp.bfloat16),
            pltpu.VMEM((*down_weight.shape[:2], half), jnp.bfloat16),
            pltpu.VMEM(up_weight.shape, jnp.bfloat16),
            pltpu.VMEM((n_inst, block, half + local), jnp.bfloat16),
            pltpu.VMEM((n_inst, block, half), jnp.bfloat16),
            pltpu.VMEM((2, steps, requests, half), jnp.bfloat16),
            pltpu.VMEM((2, 1, requests), jnp.int32),
            pltpu.VMEM((n_tp, rows, local), jnp.float32),
            pltpu.VMEM((n_tp, rows, local), jnp.float32),
            pltpu.VMEM((rank, rows), jnp.float32),
            pltpu.VMEM((rank, rows), jnp.float32),
            pltpu.VMEM((2, rank, rows), jnp.float32),
            pltpu.VMEM((n_tp, rank, rows), jnp.float32),
            pltpu.VMEM((n_tp, rank, rows), jnp.float32),
            pltpu.VMEM((rows, HEAD), jnp.float32),
            pltpu.VMEM((rows, HEAD), jnp.float32),
            pltpu.SemaphoreType.DMA((4,)),
            pltpu.SemaphoreType.DMA((6,)),
            pltpu.SemaphoreType.DMA((2, n_inst)),
            pltpu.SemaphoreType.DMA((2, n_inst)),
            pltpu.SemaphoreType.DMA((2, n_inst)),
            pltpu.SemaphoreType.DMA((2, 2)),
            pltpu.SemaphoreType.DMA((2, 2)),
            pltpu.SemaphoreType.DMA((2, n_tp)),
            pltpu.SemaphoreType.DMA((n_tp,)),
            pltpu.SemaphoreType.DMA((n_tp,)),
            pltpu.SemaphoreType.DMA((n_tp,)),
            pltpu.SemaphoreType.DMA((n_tp,)),
            pltpu.SemaphoreType.DMA((n_tp,)),
        ],
        compiler_params=pltpu.CompilerParams(
            collective_id=0, has_side_effects=True, vmem_limit_bytes=60 * 1024 * 1024
        ),
        name="lora_keys",
    )(
        pool_rows,
        request_slot.reshape(1, requests),
        lengths.reshape(1, requests),
        jnp.asarray(np.concatenate([freqs, freqs]).reshape(1, HEAD)),
        hidden,
        key_matrix,
        down_weight,
        up_weight,
    )


def solution(mesh):
    placed = (
        P(None, ("groups", "inst"), "tp"),
        P("tp", None),
        P("inst", None, "tp"),
        P("inst", None, "tp"),
        P(("groups", "inst")),
        P("groups"),
        P(("groups", "inst")),
    )
    return jax.shard_map(
        on_device,
        mesh=mesh,
        in_specs=placed,
        out_specs=P(None, ("groups", "inst"), "tp"),
        check_vma=False,
    )
```

```python
import functools

import jax
import jax.numpy as jnp
import numpy as np
from jax import lax
from jax.experimental import pallas as pl
from jax.experimental.pallas import tpu as pltpu
from jax.sharding import PartitionSpec as P

HEAD = 128
ADAPTER_SCALE = 2.0
ROPE_THETA = 500000.0
MESH_ID = pl.DeviceIdType.MESH


def rope_freqs(head_size):
    pair = np.arange(head_size // 2, dtype=np.float64)
    base = ROPE_THETA ** (-2.0 * pair / head_size)
    wavelen = 2.0 * np.pi / base
    smooth = (8192.0 / wavelen - 1.0) / 3.0
    blended = (1.0 - smooth) * base / 8.0 + smooth * base
    scaled = np.where(wavelen > 8192.0, base / 8.0, blended)
    return np.where(wavelen < 2048.0, base, scaled).astype(np.float32)


def kernel(
    n_inst, n_tp, n_act, rank, pool_rows_hbm, slot_hbm, len_hbm, freq_hbm,
    hidden_hbm, key_hbm, down_hbm, up_hbm, out_ref,
    pool_rows, slot, length, freq, hidden, key, down_low, down_high, up, low_half, high_half, guest, guest_slot,
    part, keys_in, score, total_score, help_out, help_in, score_in, cos_tab, sin_tab,
    small_sem, load_sem, out_right_sem, out_left_sem, in_sem, guest_out_sem, guest_in_sem,
    help_out_sem, help_in_sem, key_out_sem, key_in_sem, sc_out_sem, sc_in_sem,
):
    me = lax.axis_index("inst")
    tp = lax.axis_index("tp")
    _, steps, requests, half = hidden.shape
    rows = steps * requests
    local = up.shape[2]
    pool_count = down_low.shape[0]
    last = n_inst - 1
    is_end = (me == 0) | (me == last)

    load_down = [
        pltpu.make_async_copy(
            down_hbm.at[:, :, pl.ds(h * half, half)], down, load_sem.at[5 * h]
        )
        for h, down in enumerate((down_low, down_high))
    ]
    load_up = pltpu.make_async_copy(up_hbm, up, load_sem.at[1])
    load_hidden = [
        pltpu.make_async_copy(
            hidden_hbm.at[:, :, pl.ds(h * half, half)], hidden.at[h], load_sem.at[2 + h]
        )
        for h in range(2)
    ]
    load_key = pltpu.make_async_copy(key_hbm, key, load_sem.at[4])
    load_small = [
        pltpu.make_async_copy(src, dst, small_sem.at[i])
        for i, (src, dst) in enumerate(
            ((pool_rows_hbm, pool_rows), (slot_hbm, slot), (len_hbm, length), (freq_hbm, freq))
        )
    ]
    for copy in load_small:
        copy.start()
    load_down[0].start()
    load_up.start()
    load_down[1].start()

    barrier = pltpu.get_barrier_semaphore()
    for shift in (1, n_inst - 1):
        pl.semaphore_signal(
            barrier, inc=1, device_id={"inst": lax.rem(me + shift, n_inst)}, device_id_type=MESH_ID
        )
    for shift in range(1, n_tp):
        pl.semaphore_signal(
            barrier, inc=1, device_id={"tp": lax.rem(tp + shift, n_tp)}, device_id_type=MESH_ID
        )

    ends = (
        (0, 0, 1, {"inst": lax.rem(me + 1, n_inst)}),
        (1, last, last - 1, {"inst": lax.rem(me + n_inst - 1, n_inst)}),
    )
    for e, end, helper, _ in ends:
        for here, there in ((end, helper), (helper, end)):

            @pl.when(me == here)
            def _():
                for shift in range(1, n_tp):
                    pl.semaphore_signal(
                        barrier, inc=1, device_id={"inst": there, "tp": lax.rem(tp + shift, n_tp)},
                        device_id_type=MESH_ID,
                    )

    for copy in load_small:
        copy.wait()
    own_rows = [lax.rem(pool_rows[me * n_act + k], pool_count) for k in range(n_act)]
    load_down[0].wait()
    load_up.wait()
    for k, row in enumerate(own_rows):
        ranks = slice(k * rank, (k + 1) * rank)
        low_half[me, ranks, :half] = down_low[row]
        low_half[me, ranks, half:] = up[row]

    pairs = 0
    for _, end, helper, _ in ends:
        for here in (end, helper):
            pairs += jnp.where(me == here, 1, 0)
    pl.semaphore_wait(barrier, 2 + (n_tp - 1) * (1 + pairs))

    right = {"inst": lax.rem(me + 1, n_inst)}
    left = {"inst": lax.rem(me + n_inst - 1, n_inst)}

    def remote(src, dst, send_sem, recv_sem, device):
        return pltpu.make_async_remote_copy(
            src_ref=src, dst_ref=dst, send_sem=send_sem, recv_sem=recv_sem,
            device_id=device, device_id_type=MESH_ID,
        )

    def hop(h, owner, sems, device):
        buffer = high_half if h else low_half
        return remote(
            buffer.at[owner], buffer.at[owner], sems.at[h, owner], in_sem.at[h, owner], device
        )

    def go_right(h, owner):
        @pl.when(me + 1 < (last if h else n_inst))
        def _():
            hop(h, owner, out_right_sem, right).start()

    def go_left(h, owner):
        @pl.when(me > (1 if h else 0))
        def _():
            hop(h, owner, out_left_sem, left).start()

    def arrive(h, owner):
        hop(h, owner, out_right_sem, right).wait_recv()

    go_right(0, me)
    go_left(0, me)

    load_down[1].wait()
    for copy in load_hidden:
        copy.start()
    load_key.start()
    for k, row in enumerate(own_rows):
        high_half[me, k * rank : (k + 1) * rank, :] = down_high[row]

    for copy in load_hidden:
        copy.wait()
    load_key.wait()

    def send_keys(shift):
        return remote(
            part.at[shift], keys_in.at[shift], key_out_sem.at[shift], key_in_sem.at[shift],
            {"tp": lax.rem(tp + shift, n_tp)},
        )

    def partial_keys(shift):
        peer = lax.rem(tp + shift, n_tp)
        columns = pl.ds(pl.multiple_of(peer * local, local), local)
        part[shift] = jnp.dot(
            hidden[0].reshape(rows, half), key[:half, columns], preferred_element_type=jnp.float32
        ) + jnp.dot(
            hidden[1].reshape(rows, half), key[half:, columns], preferred_element_type=jnp.float32
        )

    for shift in range(1, n_tp):
        partial_keys(shift)
    partial_keys(0)

    slots = jnp.concatenate([slot[...]] * steps, axis=1)

    def pick(total, weights, values, wanted, owner):
        piece = lax.dot_general(
            weights, values, (((1,), (1,)), ((), ())), preferred_element_type=jnp.float32
        )
        for k in range(n_act):
            total += jnp.where(
                wanted == owner * n_act + k, piece[k * rank : (k + 1) * rank, :], 0.0
            )
        return total

    def add_low(owner):
        score[...] = pick(
            score[...], low_half[owner, :, :half], hidden[0].reshape(rows, half), slots, owner
        )

    def add_high(owner):
        score[...] = pick(
            score[...], high_half[owner], hidden[1].reshape(rows, half), slots, owner
        )

    score[...] = jnp.zeros((rank, rows), jnp.float32)
    add_low(me)
    add_high(me)

    lens = jnp.broadcast_to(length[...].astype(jnp.float32), (HEAD, requests)).T
    lane = lax.broadcasted_iota(jnp.int32, (requests, HEAD), 1)
    for s in range(steps):
        angle = (lens + float(s)) * freq[...]
        sine = jnp.sin(angle)
        cos_tab[s * requests : (s + 1) * requests, :] = jnp.cos(angle)
        sin_tab[s * requests : (s + 1) * requests, :] = jnp.where(lane < HEAD // 2, -sine, sine)

    @pl.when(me < last)
    def _():
        hop(0, me, out_right_sem, right).wait_send()

    go_right(1, me)

    @pl.when(me > 0)
    def _():
        hop(0, me, out_left_sem, left).wait_send()

    go_left(1, me)

    for shift in range(1, n_tp):
        send_keys(shift).start()

    def send_guest(e, device):
        return (
            remote(hidden.at[1], guest.at[e], guest_out_sem.at[e, 0], guest_in_sem.at[e, 0], device),
            remote(slot, guest_slot.at[e], guest_out_sem.at[e, 1], guest_in_sem.at[e, 1], device),
        )

    for e, end, _, device in ends:
        sems = out_left_sem if e else out_right_sem

        @pl.when(me == end)
        def _():
            if n_inst > 2:
                hop(1, me, sems, device).wait_send()
            for copy in send_guest(e, device):
                copy.start()

    def add_guest(e, owner, total):
        wanted = jnp.concatenate([guest_slot[e]] * steps, axis=1)
        return pick(total, high_half[owner], guest[e].reshape(rows, half), wanted, owner)

    def step(d, carry):
        lower = me - d
        upper = me + d
        sides = ((lower, lower >= 0, go_right), (upper, upper < n_inst, go_left))
        for owner, there, go_on in sides:

            @pl.when(there)
            def _():
                arrive(0, owner)
                go_on(0, owner)

        for owner, there, go_on in sides:

            @pl.when(there)
            def _():
                add_low(owner)

        for e, end, helper, device in ends:

            @pl.when((me == helper) & (d == max(n_inst - 2, 1)))
            def _():
                for copy in send_guest(e, device):
                    copy.wait_recv()
                help_out[e] = lax.fori_loop(
                    1, n_inst - 1, functools.partial(add_guest, e),
                    jnp.zeros((rank, rows), jnp.float32),
                )

        for owner, there, go_on in sides:

            @pl.when(there & jnp.logical_not(is_end))
            def _():
                arrive(1, owner)
                go_on(1, owner)
                add_high(owner)

        return carry

    lax.fori_loop(1, n_inst, step, 0)

    def send_help(e, shift):
        return remote(
            help_out.at[e], help_in.at[shift], help_out_sem.at[e, shift], help_in_sem.at[shift],
            {"inst": ends[e][1], "tp": lax.rem(tp + shift, n_tp)},
        )

    for e, end, helper, device in ends:

        @pl.when(me == helper)
        def _():
            help_out[e] = add_guest(e, 0 if e else last, help_out[e])
            for shift in range(n_tp):
                send_help(e, shift).start()

    def send_score(shift):
        return remote(
            score, score_in.at[shift], sc_out_sem.at[shift], sc_in_sem.at[shift],
            {"tp": lax.rem(tp + shift, n_tp)},
        )

    for shift in range(1, n_tp):
        send_score(shift).start()

    for shift in range(1, n_tp):
        send_keys(shift).wait_recv()
        part[0] += keys_in[shift]

    for shift in range(1, n_tp):
        send_score(shift).wait_recv()
    shrink = score[...]
    for shift in range(1, n_tp):
        shrink += score_in[shift]
    total_score[...] = shrink

    @pl.when(is_end)
    def _():
        for shift in range(n_tp):
            send_help(0, shift).wait_recv()
            total_score[...] += help_in[shift]

    shrink = total_score[...].astype(jnp.bfloat16).astype(jnp.float32)

    def add_update(owner, total):
        spread = jnp.concatenate(
            [jnp.where(slots == owner * n_act + k, shrink, 0.0) for k in range(n_act)], axis=0
        )
        return total + lax.dot_general(
            spread.astype(jnp.bfloat16), low_half[owner, :, half:],
            (((0,), (0,)), ((), ())), preferred_element_type=jnp.float32,
        )

    update = lax.fori_loop(0, n_inst, add_update, jnp.zeros((rows, local), jnp.float32), unroll=n_inst <= 4)
    mixed = part[0] + ADAPTER_SCALE * update.astype(jnp.bfloat16).astype(jnp.float32)
    for h in range(local // HEAD):
        values = mixed[:, h * HEAD : (h + 1) * HEAD]
        turned = values * cos_tab[...] + pltpu.roll(values, HEAD // 2, 1) * sin_tab[...]
        out_ref[:, :, h * HEAD : (h + 1) * HEAD] = turned.astype(jnp.bfloat16).reshape(
            steps, requests, HEAD
        )

    for shift in range(1, n_tp):
        send_keys(shift).wait_send()
        send_score(shift).wait_send()
    for e, end, helper, device in ends:

        @pl.when(me == end)
        def _():
            for copy in send_guest(e, device):
                copy.wait_send()

        @pl.when(me == helper)
        def _():
            for shift in range(n_tp):
                send_help(e, shift).wait_send()

    def drain(owner, carry):
        @pl.when((owner < me) & (me < last))
        def _():
            hop(0, owner, out_right_sem, right).wait_send()

        @pl.when((owner > me) & (me > 0))
        def _():
            hop(0, owner, out_left_sem, left).wait_send()

        @pl.when((owner <= me) & (me + 1 < last) & (me > 0))
        def _():
            hop(1, owner, out_right_sem, right).wait_send()

        @pl.when((owner >= me) & (me > 1) & (me < last))
        def _():
            hop(1, owner, out_left_sem, left).wait_send()

        return carry

    lax.fori_loop(0, n_inst, drain, 0)


def on_device(
    hidden, key_matrix, down_weight, up_weight, request_slot, pool_rows, lengths
):
    n_inst = lax.axis_size("inst")
    n_tp = lax.axis_size("tp")
    steps, requests, width = hidden.shape
    _, rank, local = up_weight.shape
    n_act = pool_rows.shape[0] // n_inst
    rows = steps * requests
    block = n_act * rank
    freqs = rope_freqs(HEAD)
    half = width // 2
    vmem = pl.BlockSpec(memory_space=pltpu.VMEM)
    hbm = pl.BlockSpec(memory_space=pltpu.HBM)
    return pl.pallas_call(
        functools.partial(kernel, n_inst, n_tp, n_act, rank),
        out_shape=jax.ShapeDtypeStruct((steps, requests, local), jnp.bfloat16),
        in_specs=[hbm] * 8,
        out_specs=vmem,
        scratch_shapes=[
            pltpu.SMEM(pool_rows.shape, jnp.int32),
            pltpu.VMEM((1, requests), jnp.int32),
            pltpu.VMEM((1, requests), jnp.int32),
            pltpu.VMEM((1, HEAD), jnp.float32),
            pltpu.VMEM((2, steps, requests, half), jnp.bfloat16),
            pltpu.VMEM(key_matrix.shape, jnp.bfloat16),
            pltpu.VMEM((*down_weight.shape[:2], half), jnp.bfloat16),
            pltpu.VMEM((*down_weight.shape[:2], half), jnp.bfloat16),
            pltpu.VMEM(up_weight.shape, jnp.bfloat16),
            pltpu.VMEM((n_inst, block, half + local), jnp.bfloat16),
            pltpu.VMEM((n_inst, block, half), jnp.bfloat16),
            pltpu.VMEM((2, steps, requests, half), jnp.bfloat16),
            pltpu.VMEM((2, 1, requests), jnp.int32),
            pltpu.VMEM((n_tp, rows, local), jnp.float32),
            pltpu.VMEM((n_tp, rows, local), jnp.float32),
            pltpu.VMEM((rank, rows), jnp.float32),
            pltpu.VMEM((rank, rows), jnp.float32),
            pltpu.VMEM((2, rank, rows), jnp.float32),
            pltpu.VMEM((n_tp, rank, rows), jnp.float32),
            pltpu.VMEM((n_tp, rank, rows), jnp.float32),
            pltpu.VMEM((rows, HEAD), jnp.float32),
            pltpu.VMEM((rows, HEAD), jnp.float32),
            pltpu.SemaphoreType.DMA((4,)),
            pltpu.SemaphoreType.DMA((6,)),
            pltpu.SemaphoreType.DMA((2, n_inst)),
            pltpu.SemaphoreType.DMA((2, n_inst)),
            pltpu.SemaphoreType.DMA((2, n_inst)),
            pltpu.SemaphoreType.DMA((2, 2)),
            pltpu.SemaphoreType.DMA((2, 2)),
            pltpu.SemaphoreType.DMA((2, n_tp)),
            pltpu.SemaphoreType.DMA((n_tp,)),
            pltpu.SemaphoreType.DMA((n_tp,)),
            pltpu.SemaphoreType.DMA((n_tp,)),
            pltpu.SemaphoreType.DMA((n_tp,)),
            pltpu.SemaphoreType.DMA((n_tp,)),
        ],
        compiler_params=pltpu.CompilerParams(
            collective_id=0, has_side_effects=True, vmem_limit_bytes=60 * 1024 * 1024
        ),
        name="lora_keys",
    )(
        pool_rows,
        request_slot.reshape(1, requests),
        lengths.reshape(1, requests),
        jnp.asarray(np.concatenate([freqs, freqs]).reshape(1, HEAD)),
        hidden,
        key_matrix,
        down_weight,
        up_weight,
    )


def solution(mesh):
    placed = (
        P(None, ("groups", "inst"), "tp"),
        P("tp", None),
        P("inst", None, "tp"),
        P("inst", None, "tp"),
        P(("groups", "inst")),
        P("groups"),
        P(("groups", "inst")),
    )
    return jax.shard_map(
        on_device,
        mesh=mesh,
        in_specs=placed,
        out_specs=P(None, ("groups", "inst"), "tp"),
        check_vma=False,
    )
```
